128 devices in a mesh: gx: 8 (over z, core), gy: 16 (over y, x).
Axes of the slice: x: 4, y: 4, z: 4, core: 2. Of those that a mesh axis runs over, the one named last changes fastest.
Arguments:
- ensemble: float32 [64, 256, 16384], P(None, 'gx', 'gy'), may hold values from -15 to 15
- obs_index: int32 [65536], P(('gx', 'gy')), may hold values from 0 to 1023
- obs_scale: float32 [65536], P(('gx', 'gy')), may hold values from 0.005 to 0.15
- member_order: int32 [64], replicated, may hold values from 0 to 63, each once
Outputs:
- analysis: float32 [64, 256, 16384], P(None, 'gx', 'gy')
The draws below stay inside these ranges and needn't reach their ends.
Inputs may be any that keep to these rules, and one draw needn't show every extreme that they name: `obs_index`: entries of block d (positions d * 512 to (d + 1) * 512 - 1) are local mode numbers of that block; values may repeat. `member_order`: A permutation of 0 to 63.
All inputs are finite; a program needn't handle non-finite values.
Results may differ from the reference program's by a relative error of at most 0.0001.
Values sent between devices are 32-bit elements; how exact they have to be, the bound alone decides.
No kernel may reach another device: no remote copies, remote signals or barrier semaphores. Data moves between devices by JAX's collectives and lax.ppermute only.
A program may use at most 128 MiB of HBM per device.

```python
import math
import jax
import jax.numpy as jnp
from jax import lax

M = 64
NX = 256
NY = 256
NZ = 64
XM = 64
YM = 64
ZM = 32
OBS_DEV = 512
NS_ITERS = 18
OBS = 65536
LOCAL_MODES = 1024
N_GX = 8
N_GY = 16


def draw_ensemble(key, part):
    key = jax.random.fold_in(key, 11)
    amp_key, noise_key = jax.random.split(key, 2)
    amplitude = jnp.exp(jax.random.uniform(amp_key, (M, 1, 1), jnp.float32, math.log(0.3), math.log(3.0)))
    noise = jnp.clip(jax.random.normal(noise_key, (M, NX, NY * NZ), jnp.float32), -5.0, 5.0)
    return (amplitude * noise).astype(jnp.float32)


def draw_obs_scale(key, part):
    key = jax.random.fold_in(key, 23)
    block_count = OBS // OBS_DEV
    position = (jnp.arange(OBS, dtype=jnp.int32) // OBS_DEV).astype(jnp.float32)
    ramp = 1.0 + 2.0 * position / max(block_count - 1, 1)
    base_scale = jnp.exp(jax.random.uniform(key, (OBS,), jnp.float32, math.log(0.005), math.log(0.05)))
    return (base_scale * ramp).astype(jnp.float32)


def place_ends(array, key, smallest, largest):
    index_at = [jax.random.randint(jax.random.fold_in(key, axis), (), 0, length) for axis, length in enumerate(array.shape)]
    longest = array.shape.index(max(array.shape))
    neighbour = index_at[:longest] + [(index_at[longest] + 1) % array.shape[longest]] + index_at[longest + 1:]
    return array.at[tuple(index_at)].set(smallest).at[tuple(neighbour)].set(largest)


def setup_inputs(seed: int = 0) -> dict:
    key_of = jax.random.split(jax.random.key(seed), 5)
    return {
        "ensemble": draw_ensemble(jax.random.fold_in(key_of[4], 71), 0),
        "obs_index": place_ends(jax.random.randint(key_of[1], (OBS,), 0, LOCAL_MODES), jax.random.fold_in(key_of[1], 1), 0, LOCAL_MODES - 1).astype(jnp.int32),
        "obs_scale": draw_obs_scale(jax.random.fold_in(key_of[4], 71), 0),
        "member_order": jax.random.permutation(key_of[3], M).astype(jnp.int32),
    }


exact_mode = lax.Precision.HIGHEST

def basis_table(length, mode_count):
    points = jnp.arange(length, dtype=jnp.int32)
    orders = jnp.arange(mode_count, dtype=jnp.int32)
    half_count = mode_count // 2
    frequency = jnp.where(orders < half_count, orders, orders - half_count + 1)
    phases = (frequency[:, None] * points[None, :] % length).astype(jnp.float32) * (2.0 * math.pi / length)
    scales = jnp.where(orders == 0, math.sqrt(1.0 / length), math.sqrt(2.0 / length)).astype(jnp.float32)
    values = jnp.where((orders < half_count)[:, None], jnp.cos(phases), jnp.sin(phases))
    return (scales[:, None] * values).astype(jnp.float32)

def inverse_root(matrix):
    identity = jnp.eye(matrix.shape[0], dtype=jnp.float32)
    frobenius = jnp.sqrt(jnp.sum(matrix * matrix))

    def sweep(turn, carry):
        root_iter, inverse = carry
        step_matrix = 1.5 * identity - 0.5 * jnp.dot(inverse, root_iter, precision=exact_mode)
        return (jnp.dot(root_iter, step_matrix, precision=exact_mode), jnp.dot(step_matrix, inverse, precision=exact_mode))
    root_iter, inverse = lax.fori_loop(0, NS_ITERS, sweep, (matrix / frobenius, identity))
    return inverse / jnp.sqrt(frobenius)

def reference(ensemble, obs_index, obs_scale, member_order):
    anomalies = ensemble - lax.optimization_barrier(jnp.mean(ensemble, axis=0, keepdims=True))
    basis_x = basis_table(NX, XM)
    basis_y = basis_table(NY, YM)
    basis_z = basis_table(NZ, ZM)

    def member_modes(member_field):
        shaped = member_field.reshape(NX, NY, NZ)
        depth_done = jnp.einsum('xyz,cz->xyc', shaped, basis_z, precision=exact_mode)
        cross_done = jnp.einsum('xyc,by->xbc', depth_done, basis_y, precision=exact_mode)
        return jnp.einsum('xbc,ax->abc', cross_done, basis_x, precision=exact_mode)
    coeffs = lax.map(member_modes, anomalies)
    positions = jnp.arange(OBS, dtype=jnp.int32)
    block_of = positions // OBS_DEV
    gx_index = block_of // N_GY
    gy_index = block_of % N_GY
    row_part = YM // N_GX
    depth_part = ZM // N_GY
    depth_mode = gy_index * depth_part + obs_index // (row_part * XM)
    cross_mode = gx_index * row_part + obs_index // XM % row_part
    first_mode = obs_index % XM
    observed = coeffs[:, first_mode, cross_mode, depth_mode].T
    scaled = observed * (obs_scale / math.sqrt(M - 1))[:, None]
    precision_matrix = jnp.eye(M, dtype=jnp.float32) + jnp.dot(scaled.T, scaled, precision=exact_mode, preferred_element_type=jnp.float32)
    transform = inverse_root(precision_matrix)
    weights = transform[:, member_order]
    flat_field = anomalies.reshape(M, NX * NY * NZ)
    analysis = jnp.dot(weights.T, flat_field, precision=exact_mode, preferred_element_type=jnp.float32)
    return analysis.reshape(M, NX, NY * NZ)
```

```python
import math

import jax
import jax.numpy as jnp
import numpy as np
from jax import lax
from jax.experimental import pallas as pl
from jax.experimental.pallas import tpu as pltpu
from jax.sharding import PartitionSpec as P

M = 64
NX = 256
NY = 256
NZ = 64
XM = 64
YM = 64
ZM = 32
NS_ITERS = 18
OBS_DEV = 512
GX = 8
GY = 16
LX = NX // GX
LY = NY // GY

exact_mode = lax.Precision.HIGHEST
f32 = jnp.float32
bf16 = jnp.bfloat16


def basis(length, count):
    q = np.arange(length)
    r = np.arange(count)
    half = count // 2
    freq = np.where(r < half, r, r - half + 1)
    phase = (freq[:, None] * q[None, :] % length) * (2.0 * math.pi / length)
    scale = np.where(r == 0, math.sqrt(1.0 / length), math.sqrt(2.0 / length))
    return scale[:, None] * np.where((r < half)[:, None], np.cos(phase), np.sin(phase))


def two_parts(table, axis):
    high = table.astype(np.float32).astype(jnp.bfloat16)
    low = (table - high.astype(np.float64)).astype(np.float32).astype(jnp.bfloat16)
    return np.concatenate([high, low], axis=axis)


def depth_tables():
    bz = basis(NZ, ZM)
    out = np.zeros((GX, 128, 256))
    for g in range(GX):
        for y4 in range(4):
            cols = slice(64 * y4, 64 * y4 + 64)
            for h in range(GY):
                out[g, 16 * y4 + h, cols] = bz[2 * h + 1]
            for s in range(GX):
                for c2 in range(2):
                    out[g, 64 + 8 * s + 2 * y4 + c2, cols] = bz[4 * ((g + s) % GX) + 2 * c2]
    return two_parts(out, 1)


def first_tables():
    bx = basis(NX, XM)
    out = np.zeros((GX, 2, XM, GX, LX // 2))
    for g in range(GX):
        for s in range(GX):
            start = LX * ((g - s) % GX)
            block = bx[:, start : start + LX]
            out[g, 0, :, s, :] = block[:, 0::2]
            out[g, 1, :, s, :] = block[:, 1::2]
    return two_parts(out.reshape(GX, 2 * XM, GX * LX // 2), 1)


def second_tables():
    by = basis(NY, YM)
    out = np.stack(
        [np.concatenate([by[8 * ((g + s) % GX) :][:8] for s in range(GX)]) for g in range(GX)]
    )
    return two_parts(out, 1)


def split(value):
    high = value.astype(bf16)
    return high, (value - high.astype(f32)).astype(bf16)


def three_parts(value):
    high = value.astype(bf16)
    rest = value - high.astype(f32)
    middle = rest.astype(bf16)
    return high, middle, (rest - middle.astype(f32)).astype(bf16)


def contract(table, value, dims):
    rows = table.shape[0] // 2
    high, low = split(value)
    first = lax.dot_general(table, high, (dims, ((), ())), preferred_element_type=f32)
    second = lax.dot_general(table[:rows], low, (dims, ((), ())), preferred_element_type=f32)
    return first[:rows] + first[rows:] + second


NN = ((1,), (0,))
NT = ((1,), (1,))


def half_lanes(shape):
    return lax.broadcasted_iota(jnp.int32, shape, 1) < 64


def mode_weights(index, scale):
    square = scale * (1.0 / math.sqrt(M - 1))
    square = square * square
    high = lax.broadcasted_iota(jnp.int32, (16, OBS_DEV), 0) == (index >> 6)
    low = lax.broadcasted_iota(jnp.int32, (XM, OBS_DEV), 0) == (index & 63)
    parts = jnp.concatenate(
        [jnp.where(high, part.astype(f32), 0.0) for part in three_parts(square)]
    ).astype(bf16)
    sums = lax.dot_general(
        parts, low.astype(f32).astype(bf16), (NT, ((), ())), preferred_element_type=f32
    )
    return sums[:16] + sums[16:32] + sums[32:]


def depth_kernel(place, *refs):
    del place
    tiles, table_ref, index, scale = refs[:8], refs[8], refs[9], refs[10]
    cross_ref, odd_weight, row_refs = refs[11], refs[12], refs[13:]
    step = pl.program_id(0)

    @pl.when(step == 0)
    def _():
        weight = mode_weights(index[...], scale[...])
        weight = jnp.concatenate([weight, jnp.zeros((16, 64), f32)], axis=1)
        odd_weight[...] = weight[8:]
        for ref in row_refs:
            ref[512:520, :] = weight[:8]

    means = [jnp.sum(tile[...], axis=0) * (1.0 / M) for tile in tiles]
    flats = [tile.reshape(M * 8, 128) for tile in tiles]
    cross = cross_ref.reshape(GY * 4 * LY, 128)
    table = table_ref[0]
    for group in range(2):
        for quad in range(4):
            block = jnp.concatenate(
                [
                    jnp.concatenate(
                        [
                            flats[t][pl.ds(x, M, stride=8), :] - means[t][x : x + 1]
                            for t in (2 * quad, 2 * quad + 1)
                        ],
                        axis=1,
                    )
                    for x in range(4 * group, 4 * group + 4)
                ]
            )
            modes = contract(table, block, NT)
            for pair in range(2):
                lanes = slice(128 * pair, 128 * pair + 128)
                p = 2 * group + pair
                for y4 in range(4):
                    cross[pl.ds(LY * p + 4 * quad + y4, GY, stride=4 * LY), :] = modes[
                        16 * y4 : 16 * y4 + 16, lanes
                    ]
                for shift in range(GX):
                    start = pl.multiple_of(128 * step + 32 * p + 8 * quad, 8)
                    row_refs[shift][pl.ds(start, 8), :] = modes[
                        64 + 8 * shift : 72 + 8 * shift, lanes
                    ]


def depth_modes(place, ensemble, tables, index, scale):
    tile = lambda t: pl.BlockSpec((M, 8, 128), lambda i, place: (0, i, t))
    grid_spec = pltpu.PrefetchScalarGridSpec(
        num_scalar_prefetch=1,
        grid=(LX // 8,),
        in_specs=[tile(t) for t in range(8)]
        + [pl.BlockSpec((1, 256, 256), lambda i, place: (place[0], 0, 0))]
        + [pl.BlockSpec((1, OBS_DEV), lambda i, place: (0, 0))] * 2,
        out_specs=[
            pl.BlockSpec((GY, 4, LY, 128), lambda i, place: (0, i, 0, 0)),
            pl.BlockSpec((8, 128), lambda i, place: (0, 0)),
        ]
        + [pl.BlockSpec((520, 128), lambda i, place: (0, 0))] * GX,
    )
    return pl.pallas_call(
        depth_kernel,
        grid_spec=grid_spec,
        out_shape=[pltpu.HBM((GY, LX // 2, LY, 128), f32), pltpu.HBM((8, 128), f32)]
        + [pltpu.HBM((520, 128), f32)] * GX,
        compiler_params=pltpu.CompilerParams(vmem_limit_bytes=48 << 20),
        name="depth_modes",
    )(place, *[ensemble] * 8, tables, index, scale)


def first_kernel(place, table_ref, *refs):
    blocks, out_ref, held = refs[:GX], refs[GX], refs[GX + 1]
    out = out_ref.reshape(XM * 18, 128)
    held[64:, :] = jnp.zeros((64, 128), f32)
    for shift in range(GX):
        start = pl.multiple_of(8 * ((place[0] + GX - shift) % GX), 8)
        held[pl.ds(start, 8), :] = blocks[shift][512:520, :]
    out[pl.ds(16, XM, stride=18), :] = held[...].T[:64]
    out[pl.ds(17, XM, stride=18), :] = jnp.zeros((XM, 128), f32)
    table = table_ref[0]
    left = half_lanes((XM, 128))
    for y in range(LY):
        value = jnp.concatenate(
            [
                jnp.concatenate([b[pl.ds(2 * y + c2, 16, stride=32), :] for b in blocks])
                for c2 in range(2)
            ],
            axis=1,
        )
        both = contract(table, value, NN)
        even, odd = both[:, :128], both[:, 128:]
        out[pl.ds(y, XM, stride=18), :] = jnp.where(
            left,
            even[:XM] + pltpu.roll(even[XM:], 64, 1),
            pltpu.roll(odd[:XM], 64, 1) + odd[XM:],
        )


def first_modes(place, tables, blocks):
    grid_spec = pltpu.PrefetchScalarGridSpec(
        num_scalar_prefetch=1,
        grid=(1,),
        in_specs=[pl.BlockSpec((1, 256, 128), lambda i, place: (place[0], 0, 0))]
        + [pl.BlockSpec((520, 128), lambda i, place: (0, 0))] * GX,
        out_specs=pl.BlockSpec((GY, 72, 128), lambda i, place: (0, 0, 0)),
        scratch_shapes=[pltpu.VMEM((128, 128), f32)],
    )
    return pl.pallas_call(
        first_kernel,
        grid_spec=grid_spec,
        out_shape=pltpu.HBM((GY, 72, 128), f32),
        compiler_params=pltpu.CompilerParams(vmem_limit_bytes=32 << 20),
        name="first_modes",
    )(place, tables, *blocks)


def second_kernel(place, table_ref, cross, *outs):
    del place
    step = pl.program_id(0)
    table = table_ref[0]
    for half in range(2):
        value = jnp.concatenate(
            [
                jnp.concatenate([cross[h, 2 * half + pair] for h in range(GY)])
                for pair in range(2)
            ],
            axis=1,
        )
        modes = contract(table, value, NN)
        for pair in range(2):
            for shift in range(GX):
                outs[shift].reshape(128, 128)[
                    pl.ds(4 * step + 2 * half + pair, 8, stride=16), :
                ] = modes[8 * shift : 8 * shift + 8, 128 * pair : 128 * pair + 128]


def second_modes(place, tables, cross):
    grid_spec = pltpu.PrefetchScalarGridSpec(
        num_scalar_prefetch=1,
        grid=(4,),
        in_specs=[
            pl.BlockSpec((1, 128, 256), lambda i, place: (place[0], 0, 0)),
            pl.BlockSpec((GY, 4, LY, 128), lambda i, place: (0, i, 0, 0)),
        ],
        out_specs=[pl.BlockSpec((8, 16, 128), lambda i, place: (0, 0, 0))] * GX,
    )
    return pl.pallas_call(
        second_kernel,
        grid_spec=grid_spec,
        out_shape=[pltpu.HBM((8, 16, 128), f32)] * GX,
        compiler_params=pltpu.CompilerParams(vmem_limit_bytes=32 << 20),
        name="second_modes",
    )(place, tables, cross)


def gram_kernel(place, first_table, second_table, odd_weight, even_ref, *refs):
    odd_refs, out = refs[:GX], refs[GX]
    left = half_lanes((64, 128))
    total = jnp.zeros((128, 128), f32)

    def add(rows, one, two):
        top = lax.broadcasted_iota(jnp.int32, (128, 256), 0) < 64
        weight = jnp.where(top, jnp.concatenate(one, axis=1), jnp.concatenate(two, axis=1))
        return jnp.dot(
            rows.T * weight, rows, precision=exact_mode, preferred_element_type=f32
        )

    table = second_table[...]
    rows = []
    for pair in range(2):
        value = jnp.concatenate(
            [
                jnp.concatenate([even_ref[h, 18 * a : 18 * a + 16] for h in range(GY)])
                for a in (2 * pair, 2 * pair + 1)
            ],
            axis=1,
        )
        modes = contract(table, value, NN)
        rows += [modes[:, :128], modes[:, 128:]]
    weights = [
        [even_ref[2 * place[0] + c2, 18 * a + 16 : 18 * a + 17, :64] for a in range(4)]
        for c2 in range(2)
    ]
    total += add(jnp.concatenate(rows), *weights)
    table = first_table[0]
    rows = []
    for pair in range(4):
        value = jnp.concatenate(
            [
                jnp.concatenate([ref[b] for ref in odd_refs])
                for b in (2 * pair, 2 * pair + 1)
            ],
            axis=1,
        )
        both = contract(table, value, NN)
        one, two = both[:, :128], both[:, 128:]
        rows.append(
            jnp.where(
                left,
                one[:XM] + pltpu.roll(one[XM:], 64, 1),
                pltpu.roll(two[:XM], 64, 1) + two[XM:],
            )
        )
    weights = [[odd_weight[b : b + 1, :64] for b in range(b2, 8, 2)] for b2 in range(2)]
    total += add(jnp.concatenate(rows), *weights)
    gram = total[:64] + pltpu.roll(total[64:], 64, 1)
    packed = jnp.where(half_lanes((32, 128)), gram[:32], pltpu.roll(gram[32:], 64, 1))
    for i in range(GY):
        out[i] = packed


def gram(place, first_table, second_table, odd_weight, even, odd):
    whole = lambda *shape: pl.BlockSpec(shape, lambda i, place: (0,) * len(shape))
    grid_spec = pltpu.PrefetchScalarGridSpec(
        num_scalar_prefetch=1,
        grid=(1,),
        in_specs=[
            pl.BlockSpec((1, 256, 128), lambda i, place: (place[0], 0, 0)),
            whole(128, 256),
            whole(8, 128),
            whole(GY, 72, 128),
        ]
        + [whole(8, 16, 128)] * GX,
        out_specs=whole(GY, 32, 128),
    )
    return pl.pallas_call(
        gram_kernel,
        grid_spec=grid_spec,
        out_shape=pltpu.HBM((GY, 32, 128), f32),
        compiler_params=pltpu.CompilerParams(vmem_limit_bytes=32 << 20),
        name="gram",
    )(place, first_table, second_table, odd_weight, even, *odd)


def add_kernel(parts, out):
    total = jnp.sum(parts[...], axis=0)
    for i in range(GX):
        out[i] = total


def add_parts(parts):
    return pl.pallas_call(
        add_kernel, out_shape=pltpu.HBM((GX, 32, 128), f32), name="add_parts"
    )(parts)


def exact_dot(one, two):
    a, b, c = three_parts(one)
    d, e, f = three_parts(two)
    first = jnp.dot(
        jnp.concatenate([a, a, b, a], axis=1),
        jnp.concatenate([d, e, d, f]),
        preferred_element_type=f32,
    )
    second = jnp.dot(
        jnp.concatenate([b, c], axis=1), jnp.concatenate([e, d]), preferred_element_type=f32
    )
    return first + second


def combine_table(parts, order):
    packed = jnp.sum(parts, axis=0)
    row = lax.broadcasted_iota(jnp.int32, (M, M), 0)
    column = lax.broadcasted_iota(jnp.int32, (M, M), 1)
    identity = (row == column).astype(f32)
    matrix = identity + jnp.concatenate([packed[:, :64], packed[:, 64:]])
    squares = jnp.sum(jnp.sum(matrix * matrix, axis=1, keepdims=True), axis=0, keepdims=True)
    frobenius = jnp.sqrt(squares)

    def sweep(turn, carry):
        root, inverse = carry
        change = 1.5 * identity - 0.5 * exact_dot(inverse, root)
        return exact_dot(root, change), exact_dot(change, inverse)

    _, inverse = lax.fori_loop(0, NS_ITERS, sweep, (matrix / frobenius, identity))
    transform = inverse / jnp.sqrt(frobenius)
    chosen = (order == column).astype(f32)
    weight = lax.dot_general(
        chosen, transform, (NT, ((), ())), precision=exact_mode, preferred_element_type=f32
    )
    high, low = split(weight)
    high, low = high.astype(f32), low.astype(f32)
    none = jnp.zeros((M, M), f32)
    return jnp.concatenate(
        [
            jnp.concatenate([high, high, none, none], axis=1),
            jnp.concatenate([low, none, none, none], axis=1),
            jnp.concatenate([none, none, high, high], axis=1),
            jnp.concatenate([none, none, low, none], axis=1),
        ]
    ).astype(bf16)


def analysis_kernel(parts, order, ens_hbm, out_hbm, ens, out, weights, fetched, stored):
    def fetch(n):
        i, t = n // 8, n % 8
        place = (slice(None), pl.ds(8 * i, 8), pl.ds(128 * t, 128))
        return pltpu.make_async_copy(ens_hbm.at[place], ens.at[n], fetched.at[n])

    def store(n):
        i, t = n // 8, n % 8
        place = (slice(None), pl.ds(8 * i, 8), pl.ds(128 * t, 128))
        return pltpu.make_async_copy(out.at[n], out_hbm.at[place], stored.at[n])

    count = LX * LY * NZ // 1024
    for n in range(count):
        fetch(n).start()
    weights[...] = combine_table(parts[...], order[...])

    @pl.loop(0, count // 2)
    def _(turn):
        table = weights[...]
        tiles = (2 * turn, 2 * turn + 1)
        for n in tiles:
            fetch(n).wait()
        means = [jnp.sum(ens[n], axis=0) * (1.0 / M) for n in tiles]
        flats = [ens.at[n].reshape(M * 8, 128) for n in tiles]
        outs = [out.at[n].reshape(M * 8, 128) for n in tiles]
        for x in range(0, 8, 2):
            value = []
            for i in (x, x + 1):
                value += split(
                    jnp.concatenate(
                        [flats[k][pl.ds(i, M, stride=8), :] - means[k][i : i + 1] for k in range(2)],
                        axis=1,
                    )
                )
            result = jnp.dot(table, jnp.concatenate(value), preferred_element_type=f32)
            for i in range(2):
                sums = result[128 * i : 128 * i + 64] + result[128 * i + 64 : 128 * i + 128]
                for k in range(2):
                    outs[k][pl.ds(x + i, M, stride=8), :] = sums[:, 128 * k : 128 * k + 128]
        for n in tiles:
            store(n).start()

    for n in range(count):
        store(n).wait()


def analyse(parts, order, ensemble):
    count = LX * LY * NZ // 1024
    return pl.pallas_call(
        analysis_kernel,
        in_specs=[
            pl.BlockSpec(memory_space=pltpu.VMEM),
            pl.BlockSpec(memory_space=pltpu.VMEM),
            pl.BlockSpec(memory_space=pl.ANY),
        ],
        out_specs=pl.BlockSpec(memory_space=pl.ANY),
        out_shape=jax.ShapeDtypeStruct((M, LX, LY * NZ), f32),
        scratch_shapes=[
            pltpu.VMEM((count, M, 8, 128), f32),
            pltpu.VMEM((count, M, 8, 128), f32),
            pltpu.VMEM((256, 256), bf16),
            pltpu.SemaphoreType.DMA((count,)),
            pltpu.SemaphoreType.DMA((count,)),
        ],
        compiler_params=pltpu.CompilerParams(vmem_limit_bytes=40 << 20),
        name="analysis",
    )(parts, order, ensemble)


def shifted(block, shift):
    return lax.ppermute(block, "gx", [(i, (i + shift) % GX) for i in range(GX)])


def on_device(ensemble, obs_index, obs_scale, member_order):
    gx = lax.axis_index("gx")
    place = gx.astype(jnp.int32).reshape(1)
    ensemble = pltpu.with_memory_space_constraint(ensemble, pltpu.HBM)
    first_table = jnp.asarray(first_tables())
    cross, odd_weight, *rows = depth_modes(
        place,
        ensemble,
        jnp.asarray(depth_tables()),
        obs_index.reshape(1, OBS_DEV),
        obs_scale.reshape(1, OBS_DEV),
    )
    cross = lax.all_to_all(cross, "gy", split_axis=0, concat_axis=0, tiled=True)
    rows = [rows[0]] + [shifted(rows[s], s) for s in range(1, GX)]

    even = first_modes(place, first_table, rows)
    even = lax.all_to_all(even, "gy", split_axis=0, concat_axis=0, tiled=True)
    odd = second_modes(place, jnp.asarray(second_tables()), cross)
    odd = [odd[0]] + [shifted(odd[s], s) for s in range(1, GX)]

    second_table = jnp.asarray(two_parts(basis(NY, YM), 0))
    parts = gram(place, first_table, second_table, odd_weight, even, odd)
    parts = lax.all_to_all(parts, "gy", split_axis=0, concat_axis=0, tiled=True)
    parts = add_parts(parts)
    parts = lax.all_to_all(parts, "gx", split_axis=0, concat_axis=0, tiled=True)
    return analyse(parts, member_order.reshape(M, 1), ensemble)


def solution(mesh):
    placed = (P(None, "gx", "gy"), P(("gx", "gy")), P(("gx", "gy")), P())
    return jax.shard_map(
        on_device, mesh=mesh, in_specs=placed, out_specs=P(None, "gx", "gy"), check_vma=False
    )
```

```python
import math

import jax
import jax.numpy as jnp
import numpy as np
from jax import lax
from jax.experimental import pallas as pl
from jax.experimental.pallas import tpu as pltpu
from jax.sharding import PartitionSpec as P

M = 64
NX = 256
NY = 256
NZ = 64
XM = 64
YM = 64
ZM = 32
NS_ITERS = 18
OBS_DEV = 512
GX = 8
GY = 16
LX = NX // GX
LY = NY // GY

exact_mode = lax.Precision.HIGHEST
f32 = jnp.float32
bf16 = jnp.bfloat16


def basis(length, count):
    q = np.arange(length)
    r = np.arange(count)
    half = count // 2
    freq = np.where(r < half, r, r - half + 1)
    phase = (freq[:, None] * q[None, :] % length) * (2.0 * math.pi / length)
    scale = np.where(r == 0, math.sqrt(1.0 / length), math.sqrt(2.0 / length))
    return scale[:, None] * np.where((r < half)[:, None], np.cos(phase), np.sin(phase))


def two_parts(table, axis):
    high = table.astype(np.float32).astype(jnp.bfloat16)
    low = (table - high.astype(np.float64)).astype(np.float32).astype(jnp.bfloat16)
    return np.concatenate([high, low], axis=axis)


def depth_tables():
    bz = basis(NZ, ZM)
    out = np.zeros((GX, 128, 256))
    for g in range(GX):
        for y4 in range(4):
            cols = slice(64 * y4, 64 * y4 + 64)
            for h in range(GY):
                out[g, 16 * y4 + h, cols] = bz[2 * h + 1]
            for s in range(GX):
                for c2 in range(2):
                    out[g, 64 + 8 * s + 2 * y4 + c2, cols] = bz[4 * ((g + s) % GX) + 2 * c2]
    return two_parts(out.transpose(0, 2, 1), 2)


def first_tables():
    bx = basis(NX, XM)
    out = np.zeros((GX, XM, 2, GX, LX // 2))
    for g in range(GX):
        for s in range(GX):
            start = LX * ((g - s) % GX)
            block = bx[:, start : start + LX]
            out[g, :, 0, s, :] = block[:, 0::2]
            out[g, :, 1, s, :] = block[:, 1::2]
    return two_parts(out.reshape(GX, XM, NX), 1)


def second_table():
    high, low = np.split(two_parts(basis(NY, YM), 0), 2)
    return np.stack([np.concatenate([part, part]) for part in (high, low)]).astype(np.float32)


def from_row(table, start):
    return jnp.concatenate([table[part, pl.ds(start, YM), :] for part in range(2)]).astype(bf16)


def split(value):
    high = value.astype(bf16)
    return high, (value - high.astype(f32)).astype(bf16)


def three_parts(value):
    high = value.astype(bf16)
    rest = value - high.astype(f32)
    middle = rest.astype(bf16)
    return high, middle, (rest - middle.astype(f32)).astype(bf16)


def contract(table, value):
    rows = table.shape[0] // 2
    high, low = split(value)
    first = jnp.dot(table, high, preferred_element_type=f32)
    second = jnp.dot(table[:rows], low, preferred_element_type=f32)
    return first[:rows] + first[rows:] + second


NT = ((1,), (1,))


SCALAR = pl.BlockSpec(memory_space=pltpu.SMEM)
WHOLE = pl.BlockSpec(memory_space=pltpu.VMEM)


def half_lanes(shape):
    return lax.broadcasted_iota(jnp.int32, shape, 1) < 64


def unpair(one, two):
    left = half_lanes(one.shape)
    return jnp.concatenate(
        [
            jnp.where(left, one, pltpu.roll(two, 64, 1)),
            jnp.where(left, pltpu.roll(one, 64, 1), two),
        ]
    )


def mode_weights(index, scale):
    square = scale * (1.0 / math.sqrt(M - 1))
    square = square * square
    high = lax.broadcasted_iota(jnp.int32, (16, OBS_DEV), 0) == (index >> 6)
    low = lax.broadcasted_iota(jnp.int32, (XM, OBS_DEV), 0) == (index & 63)
    parts = jnp.concatenate(
        [jnp.where(high, part.astype(f32), 0.0) for part in three_parts(square)]
    ).astype(bf16)
    sums = lax.dot_general(
        parts, low.astype(f32).astype(bf16), (NT, ((), ())), preferred_element_type=f32
    )
    return sums[:16] + sums[16:32] + sums[32:]


def one_row(ref):
    return jnp.concatenate([ref[i : i + 1, :] for i in range(OBS_DEV // 128)], axis=1)


def depth_kernel(place, ens, table_ref, index, scale, cross_ref, odd_weight, *refs):
    del place
    row_refs, held = refs[:GX], refs[GX]
    step = pl.program_id(0)

    @pl.when(step == 0)
    def _():
        weight = mode_weights(one_row(index), one_row(scale))
        weight = jnp.concatenate([weight, jnp.zeros((16, 64), f32)], axis=1)
        odd_weight[...] = weight[8:]
        for ref in row_refs:
            ref[512:520, :] = weight[:8]

    cross = cross_ref.reshape(GY * 4 * LY, 128)
    table = table_ref[0]
    for quad in range(4):
        lanes = slice(256 * quad, 256 * quad + 256)
        block = ens[:, :, lanes]
        block = (block - jnp.sum(block, axis=0, keepdims=True) * (1.0 / M)).reshape(M * 8, 256)
        high, low = split(block)
        first = jnp.dot(high, table, preferred_element_type=f32)
        second = jnp.dot(low, table[:, :128], preferred_element_type=f32)
        held[quad] = first[:, :128] + first[:, 128:] + second
        for p in range(4):
            modes = jnp.concatenate(
                [held[quad, pl.ds(2 * p + parity, M, stride=8), :] for parity in range(2)]
            ).T
            for y4 in range(4):
                cross[pl.ds(LY * p + 4 * quad + y4, GY, stride=4 * LY), :] = modes[
                    16 * y4 : 16 * y4 + 16
                ]
            for shift in range(GX):
                start = pl.multiple_of(128 * step + 32 * p + 8 * quad, 8)
                row_refs[shift][pl.ds(start, 8), :] = modes[64 + 8 * shift : 72 + 8 * shift]


def depth_modes(place, ensemble, tables, index, scale):
    grid_spec = pltpu.PrefetchScalarGridSpec(
        num_scalar_prefetch=1,
        grid=(LX // 8,),
        in_specs=[pl.BlockSpec((M, 8, LY * NZ), lambda i, place: (0, i, 0))]
        + [pl.BlockSpec((1, 256, 256), lambda i, place: (place[0], 0, 0))]
        + [pl.BlockSpec((OBS_DEV // 128, 128), lambda i, place: (0, 0))] * 2,
        out_specs=[
            pl.BlockSpec((GY, 4, LY, 128), lambda i, place: (0, i, 0, 0)),
            pl.BlockSpec((8, 128), lambda i, place: (0, 0)),
        ]
        + [pl.BlockSpec((520, 128), lambda i, place: (0, 0))] * GX,
        scratch_shapes=[pltpu.VMEM((4, M * 8, 128), f32)],
    )
    return pl.pallas_call(
        depth_kernel,
        grid_spec=grid_spec,
        out_shape=[pltpu.HBM((GY, LX // 2, LY, 128), f32)]
        + [jax.ShapeDtypeStruct(shape, f32) for shape in ((8, 128), (520, 128))]
        + [pltpu.HBM((520, 128), f32)] * (GX - 1),
        compiler_params=pltpu.CompilerParams(vmem_limit_bytes=48 << 20),
        name="depth_modes",
    )(place, ensemble, tables, index, scale)


def first_kernel(place, table_ref, *refs):
    blocks, out_ref, held = refs[:GX], refs[GX], refs[GX + 1]
    out = out_ref.reshape(XM * 18, 128)
    held[64:, :] = jnp.zeros((64, 128), f32)
    for shift in range(GX):
        start = pl.multiple_of(8 * ((place[0] + GX - shift) % GX), 8)
        held[pl.ds(start, 8), :] = blocks[shift][512:520, :]
    out[pl.ds(16, XM, stride=18), :] = held[...].T[:64]
    out[pl.ds(17, XM, stride=18), :] = jnp.zeros((XM, 128), f32)
    table = table_ref[place[0]]
    for y in range(0, LY, 2):
        value = [
            unpair(
                *[
                    jnp.concatenate([b[pl.ds(2 * k + c2, 16, stride=32), :] for b in blocks])
                    for c2 in range(2)
                ]
            )
            for k in (y, y + 1)
        ]
        modes = contract(table, jnp.concatenate(value, axis=1))
        for k in range(2):
            out[pl.ds(y + k, XM, stride=18), :] = modes[:, 128 * k : 128 * k + 128]


def first_modes(place, tables, blocks):
    return pl.pallas_call(
        first_kernel,
        in_specs=[SCALAR] + [WHOLE] * (GX + 1),
        out_specs=WHOLE,
        out_shape=pltpu.HBM((GY, 72, 128), f32),
        scratch_shapes=[pltpu.VMEM((128, 128), f32)],
        compiler_params=pltpu.CompilerParams(vmem_limit_bytes=16 << 20),
        name="first_modes",
    )(place, tables, *blocks)


def second_kernel(place, table_ref, cross, *outs):
    table = from_row(table_ref, pl.multiple_of(8 * place[0], 8))
    for group in range(LX // 4):
        value = jnp.concatenate(
            [
                jnp.concatenate([cross[h, 2 * group + pair] for h in range(GY)])
                for pair in range(2)
            ],
            axis=1,
        )
        modes = contract(table, value)
        for pair in range(2):
            for shift in range(GX):
                outs[shift].reshape(128, 128)[
                    pl.ds(2 * group + pair, 8, stride=16), :
                ] = modes[8 * shift : 8 * shift + 8, 128 * pair : 128 * pair + 128]


def second_modes(place, tables, cross):
    return pl.pallas_call(
        second_kernel,
        in_specs=[SCALAR, WHOLE, WHOLE],
        out_specs=[WHOLE] * GX,
        out_shape=[jax.ShapeDtypeStruct((8, 16, 128), f32)]
        + [pltpu.HBM((8, 16, 128), f32)] * (GX - 1),
        compiler_params=pltpu.CompilerParams(vmem_limit_bytes=16 << 20),
        name="second_modes",
    )(place, tables, cross)


def gram_kernel(place, first_table, table_ref, odd_weight, even_ref, *refs):
    odd_refs, out = refs[:GX], refs[GX]
    total = jnp.zeros((128, 128), f32)

    def add(rows, one, two):
        top = lax.broadcasted_iota(jnp.int32, (128, 256), 0) < 64
        weight = jnp.where(top, jnp.concatenate(one, axis=1), jnp.concatenate(two, axis=1))
        return jnp.dot(
            rows.T * weight, rows, precision=exact_mode, preferred_element_type=f32
        )

    table = from_row(table_ref, 0)
    rows = []
    for pair in range(2):
        value = jnp.concatenate(
            [
                jnp.concatenate([even_ref[h, 18 * a : 18 * a + 16] for h in range(GY)])
                for a in (2 * pair, 2 * pair + 1)
            ],
            axis=1,
        )
        modes = contract(table, value)
        rows += [modes[:, :128], modes[:, 128:]]
    weights = [
        [even_ref[2 * place[0] + c2, 18 * a + 16 : 18 * a + 17, :64] for a in range(4)]
        for c2 in range(2)
    ]
    total += add(jnp.concatenate(rows), *weights)
    table = first_table[place[0]]
    rows = []
    for b in range(0, 8, 4):
        value = [
            unpair(*[jnp.concatenate([ref[k + b2] for ref in odd_refs]) for b2 in range(2)])
            for k in (b, b + 2)
        ]
        modes = contract(table, jnp.concatenate(value, axis=1))
        rows += [modes[:, :128], modes[:, 128:]]
    weights = [[odd_weight[b : b + 1, :64] for b in range(b2, 8, 2)] for b2 in range(2)]
    total += add(jnp.concatenate(rows), *weights)
    gram = total[:64] + pltpu.roll(total[64:], 64, 1)
    packed = jnp.where(half_lanes((32, 128)), gram[:32], pltpu.roll(gram[32:], 64, 1))
    for i in range(GX):
        out[i] = packed


def gram(place, first_table, second_table, odd_weight, even, odd):
    return pl.pallas_call(
        gram_kernel,
        in_specs=[SCALAR] + [WHOLE] * (GX + 4),
        out_specs=WHOLE,
        out_shape=jax.ShapeDtypeStruct((GX, 32, 128), f32),
        compiler_params=pltpu.CompilerParams(vmem_limit_bytes=16 << 20),
        name="gram",
    )(place, first_table, second_table, odd_weight, even, *odd)


def exact_dot(one, two):
    a, b, c = three_parts(one)
    d, e, f = three_parts(two)
    first = jnp.dot(jnp.concatenate([a, b, c]), d, preferred_element_type=f32)
    second = jnp.dot(jnp.concatenate([a, b]), e, preferred_element_type=f32)
    third = jnp.dot(a, f, preferred_element_type=f32)
    return first[:M] + (second[:M] + first[M : 2 * M]) + (first[2 * M :] + second[M:] + third)


def combine_table(parts, order, beside):
    packed = jnp.sum(parts, axis=0)
    row = lax.broadcasted_iota(jnp.int32, (M, M), 0)
    column = lax.broadcasted_iota(jnp.int32, (M, M), 1)
    identity = (row == column).astype(f32)
    matrix = identity + jnp.concatenate([packed[:, :64], packed[:, 64:]])
    squares = jnp.sum(jnp.sum(matrix * matrix, axis=1, keepdims=True), axis=0, keepdims=True)
    frobenius = jnp.sqrt(squares)

    def sweep(turn, carry):
        root, inverse = carry
        change = 1.5 * identity - 0.5 * exact_dot(inverse, root)
        return exact_dot(root, change), exact_dot(change, inverse)

    def sweep_beside(turn, carry):
        beside(turn)
        return sweep(turn, carry)

    carry = lax.fori_loop(0, 16, sweep_beside, (matrix / frobenius, identity))
    _, inverse = lax.fori_loop(16, NS_ITERS, sweep, carry)
    transform = inverse / jnp.sqrt(frobenius)
    chosen = (order == row).astype(f32).T
    weight = lax.dot_general(
        chosen, transform, (NT, ((), ())), precision=exact_mode, preferred_element_type=f32
    )
    high, low = split(weight)
    high, low = high.astype(f32), low.astype(f32)
    none = jnp.zeros((M, M), f32)
    return jnp.concatenate(
        [
            jnp.concatenate([high, high, none, none], axis=1),
            jnp.concatenate([low, none, none, none], axis=1),
            jnp.concatenate([none, none, high, high], axis=1),
            jnp.concatenate([none, none, low, none], axis=1),
        ]
    ).astype(bf16)


def analysis_kernel(parts, order, ens_hbm, out_hbm, ens, ready, out, weights, fetched, stored):
    def fetch(n):
        i, t = n // 8, n % 8
        place = (slice(None), pl.ds(8 * i, 8), pl.ds(128 * t, 128))
        return pltpu.make_async_copy(ens_hbm.at[place], ens.at[n], fetched.at[n])

    def store(n):
        i, t = n // 8, n % 8
        place = (slice(None), pl.ds(8 * i, 8), pl.ds(128 * t, 128))
        return pltpu.make_async_copy(out.at[n], out_hbm.at[place], stored.at[n])

    count = LX * LY * NZ // 1024
    for n in range(count):
        fetch(n).start()

    def prepare(pair):
        tiles = (2 * pair, 2 * pair + 1)
        for n in tiles:
            fetch(n).wait()
        means = [jnp.sum(ens[n], axis=0) * (1.0 / M) for n in tiles]
        flats = [ens.at[n].reshape(M * 8, 128) for n in tiles]
        for x in range(8):
            high, low = split(
                jnp.concatenate(
                    [flats[k][pl.ds(x, M, stride=8), :] - means[k][x : x + 1] for k in range(2)],
                    axis=1,
                )
            )
            ready[4 * pair + x // 2, 128 * (x % 2) : 128 * (x % 2) + 64] = high
            ready[4 * pair + x // 2, 128 * (x % 2) + 64 : 128 * (x % 2) + 128] = low

    weights[...] = combine_table(parts[...], order[...], prepare)

    @pl.loop(0, LX // 8)
    def _(group):
        table = weights[...]
        for pair in range(4):
            tiles = (8 * group + 2 * pair, 8 * group + 2 * pair + 1)
            outs = [out.at[n].reshape(M * 8, 128) for n in tiles]
            for x in range(0, 8, 2):
                result = jnp.dot(
                    table, ready[16 * group + 4 * pair + x // 2], preferred_element_type=f32
                )
                for i in range(2):
                    sums = result[128 * i : 128 * i + 64] + result[128 * i + 64 : 128 * i + 128]
                    for k in range(2):
                        outs[k][pl.ds(x + i, M, stride=8), :] = sums[:, 128 * k : 128 * k + 128]
            for n in tiles:
                store(n).start()

    for n in range(count):
        store(n).wait()


def analyse(parts, order, ensemble):
    count = LX * LY * NZ // 1024
    return pl.pallas_call(
        analysis_kernel,
        in_specs=[
            pl.BlockSpec(memory_space=pltpu.VMEM),
            pl.BlockSpec(memory_space=pltpu.VMEM),
            pl.BlockSpec(memory_space=pl.ANY),
        ],
        out_specs=pl.BlockSpec(memory_space=pl.ANY),
        out_shape=jax.ShapeDtypeStruct((M, LX, LY * NZ), f32),
        scratch_shapes=[
            pltpu.VMEM((count, M, 8, 128), f32),
            pltpu.VMEM((2 * count, 256, 256), bf16),
            pltpu.VMEM((count, M, 8, 128), f32),
            pltpu.VMEM((256, 256), bf16),
            pltpu.SemaphoreType.DMA((count,)),
            pltpu.SemaphoreType.DMA((count,)),
        ],
        compiler_params=pltpu.CompilerParams(vmem_limit_bytes=40 << 20),
        name="analysis",
    )(parts, order, ensemble)


def shifted(block, shift):
    return lax.ppermute(block, "gx", [(i, (i + shift) % GX) for i in range(GX)])


def on_device(ensemble, obs_index, obs_scale, member_order):
    gx = lax.axis_index("gx")
    place = gx.astype(jnp.int32).reshape(1)
    ensemble = pltpu.with_memory_space_constraint(ensemble, pltpu.HBM)
    in_hbm = lambda table: pltpu.with_memory_space_constraint(jnp.asarray(table), pltpu.HBM)
    first_table = jnp.asarray(first_tables())
    y_table = jnp.asarray(second_table())
    cross, odd_weight, *rows = depth_modes(
        place,
        ensemble,
        in_hbm(depth_tables()),
        in_hbm(obs_index.reshape(OBS_DEV // 128, 128)),
        in_hbm(obs_scale.reshape(OBS_DEV // 128, 128)),
    )
    cross = lax.all_to_all(cross, "gy", split_axis=0, concat_axis=0, tiled=True)
    rows = [rows[0]] + [shifted(rows[s], s) for s in range(1, GX)]
    even = first_modes(place, first_table, rows)
    odd = second_modes(place, y_table, cross)
    even = lax.all_to_all(even, "gy", split_axis=0, concat_axis=0, tiled=True)
    odd = [odd[0]] + [shifted(odd[s], s) for s in range(1, GX)]
    parts = gram(place, first_table, y_table, odd_weight, even, odd)
    parts = lax.all_to_all(parts, "gx", split_axis=0, concat_axis=0, tiled=True)
    parts = jnp.broadcast_to(jnp.sum(parts, axis=0), (GY, 32, 128))
    parts = lax.all_to_all(parts, "gy", split_axis=0, concat_axis=0, tiled=True)
    return analyse(parts, member_order.reshape(1, M), ensemble)


def solution(mesh):
    placed = (P(None, "gx", "gy"), P(("gx", "gy")), P(("gx", "gy")), P())
    return jax.shard_map(
        on_device, mesh=mesh, in_specs=placed, out_specs=P(None, "gx", "gy"), check_vma=False
    )
```

```python
import math

import jax
import jax.numpy as jnp
import numpy as np
from jax import lax
from jax.experimental import pallas as pl
from jax.experimental.pallas import tpu as pltpu
from jax.sharding import PartitionSpec as P

M = 64
NX = 256
NY = 256
NZ = 64
XM = 64
YM = 64
ZM = 32
NS_ITERS = 18
OBS_DEV = 512
GX = 8
GY = 16
LX = NX // GX
LY = NY // GY

exact_mode = lax.Precision.HIGHEST
f32 = jnp.float32
bf16 = jnp.bfloat16


def basis(length, count):
    q = np.arange(length)
    r = np.arange(count)
    half = count // 2
    freq = np.where(r < half, r, r - half + 1)
    phase = (freq[:, None] * q[None, :] % length) * (2.0 * math.pi / length)
    scale = np.where(r == 0, math.sqrt(1.0 / length), math.sqrt(2.0 / length))
    return scale[:, None] * np.where((r < half)[:, None], np.cos(phase), np.sin(phase))


def two_parts(table, axis):
    high = table.astype(np.float32).astype(jnp.bfloat16)
    low = (table - high.astype(np.float64)).astype(np.float32).astype(jnp.bfloat16)
    return np.concatenate([high, low], axis=axis)


def depth_tables():
    bz = basis(NZ, ZM)
    out = np.zeros((GX, 128, 256))
    for g in range(GX):
        for y4 in range(4):
            cols = slice(64 * y4, 64 * y4 + 64)
            for h in range(GY):
                out[g, 16 * y4 + h, cols] = bz[2 * (GY - 1 - h) + 1]
            for s in range(GX):
                for c2 in range(2):
                    out[g, 64 + 8 * s + 2 * y4 + c2, cols] = bz[4 * ((g + s) % GX) + 2 * c2]
    return two_parts(out.transpose(0, 2, 1), 2)


def first_tables():
    bx = basis(NX, XM)
    out = np.zeros((GX, XM, GX, 2, LX // 2))
    for g in range(GX):
        for s in range(GX):
            start = LX * ((g - s) % GX)
            block = bx[:, start : start + LX]
            out[g, :, s, 0, :] = block[:, 0::2]
            out[g, :, s, 1, :] = block[:, 1::2]
    return two_parts(out.reshape(GX, XM, NX), 1)


def second_table():
    high, low = np.split(two_parts(basis(NY, YM), 0), 2)
    return np.stack([np.concatenate([part, part]) for part in (high, low)]).astype(np.float32)


def from_row(table, start):
    return jnp.concatenate([table[part, pl.ds(start, YM), :] for part in range(2)]).astype(bf16)


def split(value):
    high = value.astype(bf16)
    return high, (value - high.astype(f32)).astype(bf16)


def three_parts(value):
    high = value.astype(bf16)
    rest = value - high.astype(f32)
    middle = rest.astype(bf16)
    return high, middle, (rest - middle.astype(f32)).astype(bf16)


def contract(table, value):
    rows = table.shape[0] // 2
    high, low = split(value)
    first = jnp.dot(table, high, preferred_element_type=f32)
    second = jnp.dot(table[:rows], low, preferred_element_type=f32)
    return first[:rows] + first[rows:] + second


NT = ((1,), (1,))


SCALAR = pl.BlockSpec(memory_space=pltpu.SMEM)
WHOLE = pl.BlockSpec(memory_space=pltpu.VMEM)


def half_lanes(shape):
    return lax.broadcasted_iota(jnp.int32, shape, 1) < 64


def unpair(one, two):
    left = half_lanes(one.shape)
    return jnp.concatenate(
        [
            jnp.where(left, one, pltpu.roll(two, 64, 1)),
            jnp.where(left, pltpu.roll(one, 64, 1), two),
        ]
    )


def mode_weights(index, scale):
    square = scale * (1.0 / math.sqrt(M - 1))
    square = square * square
    high = lax.broadcasted_iota(jnp.int32, (16, OBS_DEV), 0) == (index >> 6)
    low = lax.broadcasted_iota(jnp.int32, (XM, OBS_DEV), 0) == (index & 63)
    parts = jnp.concatenate(
        [jnp.where(high, part.astype(f32), 0.0) for part in three_parts(square)]
    ).astype(bf16)
    sums = lax.dot_general(
        parts, low.astype(f32).astype(bf16), (NT, ((), ())), preferred_element_type=f32
    )
    return sums[:16] + sums[16:32] + sums[32:]


def one_row(ref):
    return jnp.concatenate([ref[i : i + 1, :] for i in range(OBS_DEV // 128)], axis=1)


def depth_kernel(place, ens, table_ref, index, scale, cross_ref, odd_weight, *refs):
    del place
    row_refs, held = refs[:GX], refs[GX]
    step = pl.program_id(0)

    @pl.when(step == 0)
    def _():
        weight = mode_weights(one_row(index), one_row(scale))
        weight = jnp.concatenate([weight, jnp.zeros((16, 64), f32)], axis=1)
        odd_weight[...] = weight[8:]
        for ref in row_refs:
            ref[512:520, :] = weight[:8]

    cross = cross_ref.reshape(GY * 4 * LY, 128)
    table = table_ref[0]
    for quad in range(4):
        lanes = slice(256 * quad, 256 * quad + 256)
        block = ens[:, :, lanes]
        block = (block - jnp.sum(block, axis=0, keepdims=True) * (1.0 / M)).reshape(M * 8, 256)
        high, low = split(block)
        first = jnp.dot(high, table, preferred_element_type=f32)
        second = jnp.dot(low, table[:, :128], preferred_element_type=f32)
        held[quad] = first[:, :128] + first[:, 128:] + second
        for p in range(4):
            modes = jnp.concatenate(
                [held[quad, pl.ds(2 * p + parity, M, stride=8), :] for parity in range(2)]
            ).T
            for y4 in range(4):
                cross[pl.ds(LY * p + 4 * quad + y4, GY, stride=4 * LY), :] = modes[
                    16 * y4 : 16 * y4 + 16
                ]
            for shift in range(GX):
                start = pl.multiple_of(128 * step + 32 * p + 8 * quad, 8)
                row_refs[shift][pl.ds(start, 8), :] = modes[64 + 8 * shift : 72 + 8 * shift]


def depth_modes(place, ensemble, tables, index, scale):
    grid_spec = pltpu.PrefetchScalarGridSpec(
        num_scalar_prefetch=1,
        grid=(LX // 8,),
        in_specs=[pl.BlockSpec((M, 8, LY * NZ), lambda i, place: (0, i, 0))]
        + [pl.BlockSpec((1, 256, 256), lambda i, place: (place[0], 0, 0))]
        + [pl.BlockSpec((OBS_DEV // 128, 128), lambda i, place: (0, 0))] * 2,
        out_specs=[
            pl.BlockSpec((GY, 4, LY, 128), lambda i, place: (0, i, 0, 0)),
            pl.BlockSpec((8, 128), lambda i, place: (0, 0)),
        ]
        + [pl.BlockSpec((520, 128), lambda i, place: (0, 0))] * GX,
        scratch_shapes=[pltpu.VMEM((4, M * 8, 128), f32)],
    )
    return pl.pallas_call(
        depth_kernel,
        grid_spec=grid_spec,
        out_shape=[pltpu.HBM((GY, LX // 2, LY, 128), f32)]
        + [jax.ShapeDtypeStruct(shape, f32) for shape in ((8, 128), (520, 128))]
        + [pltpu.HBM((520, 128), f32)] * (GX - 1),
        compiler_params=pltpu.CompilerParams(vmem_limit_bytes=48 << 20),
        name="depth_modes",
    )(place, ensemble, tables, index, scale)


def first_product(blocks, columns, table, y):
    value = [
        jnp.concatenate(
            [unpair(*[b[pl.ds(2 * k + c2, 16, stride=32), :] for c2 in range(2)]) for b in blocks]
        )
        for k in (y, y + 1)
    ]
    return contract(table[:, columns], jnp.concatenate(value, axis=1))


def first_half_kernel(place, table_ref, *refs):
    blocks, out = refs[: GX // 2], refs[GX // 2]
    table = table_ref[place[0]]
    for y in range(0, LY, 2):
        out[y // 2] = first_product(blocks, slice(0, NX // 2), table, y)


def first_kernel(place, table_ref, half, *refs):
    blocks, out_ref, held = refs[:GX], refs[GX], refs[GX + 1]
    out = out_ref.reshape(XM * 18, 128)
    held[64:, :] = jnp.zeros((64, 128), f32)
    for shift in range(GX):
        start = pl.multiple_of(8 * ((place[0] + GX - shift) % GX), 8)
        held[pl.ds(start, 8), :] = blocks[shift][512:520, :]
    out[pl.ds(16, XM, stride=18), :] = held[...].T[:64]
    out[pl.ds(17, XM, stride=18), :] = jnp.zeros((XM, 128), f32)
    table = table_ref[place[0]]
    for y in range(0, LY, 2):
        modes = half[y // 2] + first_product(blocks[GX // 2 :], slice(NX // 2, NX), table, y)
        for k in range(2):
            out[pl.ds(y + k, XM, stride=18), :] = modes[:, 128 * k : 128 * k + 128]


def first_modes(place, tables, blocks):
    params = pltpu.CompilerParams(vmem_limit_bytes=16 << 20)
    half = pl.pallas_call(
        first_half_kernel,
        in_specs=[SCALAR] + [WHOLE] * (GX // 2 + 1),
        out_specs=WHOLE,
        out_shape=jax.ShapeDtypeStruct((LY // 2, XM, 256), f32),
        compiler_params=params,
        name="first_half",
    )(place, tables, *blocks[: GX // 2])
    return pl.pallas_call(
        first_kernel,
        in_specs=[SCALAR] + [WHOLE] * (GX + 2),
        out_specs=WHOLE,
        out_shape=pltpu.HBM((GY, 72, 128), f32),
        scratch_shapes=[pltpu.VMEM((128, 128), f32)],
        compiler_params=params,
        name="first_modes",
    )(place, tables, half, *blocks)


def second_kernel(place, table_ref, cross, *outs):
    table = from_row(table_ref, pl.multiple_of(8 * place[0], 8))
    for group in range(LX // 4):
        value = jnp.concatenate(
            [
                jnp.concatenate([cross[h, 2 * group + pair] for h in reversed(range(GY))])
                for pair in range(2)
            ],
            axis=1,
        )
        modes = contract(table, value)
        for pair in range(2):
            for shift in range(GX):
                outs[shift].reshape(128, 128)[
                    pl.ds(2 * group + pair, 8, stride=16), :
                ] = modes[8 * shift : 8 * shift + 8, 128 * pair : 128 * pair + 128]


def second_modes(place, tables, cross):
    return pl.pallas_call(
        second_kernel,
        in_specs=[SCALAR, WHOLE, WHOLE],
        out_specs=[WHOLE] * GX,
        out_shape=[jax.ShapeDtypeStruct((8, 16, 128), f32)]
        + [pltpu.HBM((8, 16, 128), f32)] * (GX - 1),
        compiler_params=pltpu.CompilerParams(vmem_limit_bytes=16 << 20),
        name="second_modes",
    )(place, tables, cross)


def gram_kernel(place, first_table, table_ref, odd_weight, even_ref, *refs):
    odd_refs, out = refs[:GX], refs[GX]
    total = jnp.zeros((128, 128), f32)

    def add(rows, one, two):
        top = lax.broadcasted_iota(jnp.int32, (128, 256), 0) < 64
        weight = jnp.where(top, jnp.concatenate(one, axis=1), jnp.concatenate(two, axis=1))
        return jnp.dot(
            rows.T * weight, rows, precision=exact_mode, preferred_element_type=f32
        )

    table = from_row(table_ref, 0)
    rows = []
    for pair in range(2):
        value = jnp.concatenate(
            [
                jnp.concatenate([even_ref[h, 18 * a : 18 * a + 16] for h in range(GY)])
                for a in (2 * pair, 2 * pair + 1)
            ],
            axis=1,
        )
        modes = contract(table, value)
        rows += [modes[:, :128], modes[:, 128:]]
    weights = [
        [even_ref[2 * place[0] + c2, 18 * a + 16 : 18 * a + 17, :64] for a in range(4)]
        for c2 in range(2)
    ]
    total += add(jnp.concatenate(rows), *weights)
    table = first_table[place[0]]
    rows = []
    for b in range(0, 8, 4):
        value = [
            jnp.concatenate([unpair(*[ref[k + b2] for b2 in range(2)]) for ref in odd_refs])
            for k in (b, b + 2)
        ]
        modes = contract(table, jnp.concatenate(value, axis=1))
        rows += [modes[:, :128], modes[:, 128:]]
    weights = [[odd_weight[b : b + 1, :64] for b in range(b2, 8, 2)] for b2 in range(2)]
    total += add(jnp.concatenate(rows), *weights)
    gram = total[:64] + pltpu.roll(total[64:], 64, 1)
    packed = jnp.where(half_lanes((32, 128)), gram[:32], pltpu.roll(gram[32:], 64, 1))
    for i in range(GX):
        out[i] = packed


def gram(place, first_table, second_table, odd_weight, even, odd):
    return pl.pallas_call(
        gram_kernel,
        in_specs=[SCALAR] + [WHOLE] * (GX + 4),
        out_specs=WHOLE,
        out_shape=jax.ShapeDtypeStruct((GX, 32, 128), f32),
        compiler_params=pltpu.CompilerParams(vmem_limit_bytes=16 << 20),
        name="gram",
    )(place, first_table, second_table, odd_weight, even, *odd)


def exact_dot(one, two):
    a, b, c = three_parts(one)
    d, e, f = three_parts(two)
    first = jnp.dot(jnp.concatenate([a, b, c]), d, preferred_element_type=f32)
    second = jnp.dot(jnp.concatenate([a, b]), e, preferred_element_type=f32)
    third = jnp.dot(a, f, preferred_element_type=f32)
    return first[:M] + (second[:M] + first[M : 2 * M]) + (first[2 * M :] + second[M:] + third)


def combine_table(parts, order, beside):
    packed = jnp.sum(parts, axis=0)
    row = lax.broadcasted_iota(jnp.int32, (M, M), 0)
    column = lax.broadcasted_iota(jnp.int32, (M, M), 1)
    identity = (row == column).astype(f32)
    matrix = identity + jnp.concatenate([packed[:, :64], packed[:, 64:]])
    squares = jnp.sum(jnp.sum(matrix * matrix, axis=1, keepdims=True), axis=0, keepdims=True)
    frobenius = jnp.sqrt(squares)

    def sweep(turn, carry):
        root, inverse = carry
        change = 1.5 * identity - 0.5 * exact_dot(inverse, root)
        return exact_dot(root, change), exact_dot(change, inverse)

    def sweep_beside(turn, carry):
        beside(turn)
        return sweep(turn, carry)

    carry = lax.fori_loop(0, 16, sweep_beside, (matrix / frobenius, identity))
    _, inverse = lax.fori_loop(16, NS_ITERS, sweep, carry)
    transform = inverse / jnp.sqrt(frobenius)
    chosen = (order == row).astype(f32).T
    weight = lax.dot_general(
        chosen, transform, (NT, ((), ())), precision=exact_mode, preferred_element_type=f32
    )
    high, low = split(weight)
    high, low = high.astype(f32), low.astype(f32)
    none = jnp.zeros((M, M), f32)
    return jnp.concatenate(
        [
            jnp.concatenate([high, high, none, none], axis=1),
            jnp.concatenate([low, none, none, none], axis=1),
            jnp.concatenate([none, none, high, high], axis=1),
            jnp.concatenate([none, none, low, none], axis=1),
        ]
    ).astype(bf16)


def analysis_kernel(parts, order, ens_hbm, out_hbm, ens, ready, out, weights, fetched, stored):
    def fetch(n):
        i, t = n // 8, n % 8
        place = (slice(None), pl.ds(8 * i, 8), pl.ds(128 * t, 128))
        return pltpu.make_async_copy(ens_hbm.at[place], ens.at[n], fetched.at[n])

    def store(n):
        i, t = n // 8, n % 8
        place = (slice(None), pl.ds(8 * i, 8), pl.ds(128 * t, 128))
        return pltpu.make_async_copy(out.at[n], out_hbm.at[place], stored.at[n])

    count = LX * LY * NZ // 1024
    for n in range(count):
        fetch(n).start()

    def prepare(pair):
        tiles = (2 * pair, 2 * pair + 1)
        for n in tiles:
            fetch(n).wait()
        means = [jnp.sum(ens[n], axis=0) * (1.0 / M) for n in tiles]
        flats = [ens.at[n].reshape(M * 8, 128) for n in tiles]
        for x in range(8):
            high, low = split(
                jnp.concatenate(
                    [flats[k][pl.ds(x, M, stride=8), :] - means[k][x : x + 1] for k in range(2)],
                    axis=1,
                )
            )
            ready[4 * pair + x // 2, 128 * (x % 2) : 128 * (x % 2) + 64] = high
            ready[4 * pair + x // 2, 128 * (x % 2) + 64 : 128 * (x % 2) + 128] = low

    weights[...] = combine_table(parts[...], order[...], prepare)

    @pl.loop(0, LX // 8)
    def _(group):
        table = weights[...]
        for pair in range(4):
            tiles = (8 * group + 2 * pair, 8 * group + 2 * pair + 1)
            outs = [out.at[n].reshape(M * 8, 128) for n in tiles]
            for x in range(0, 8, 2):
                result = jnp.dot(
                    table, ready[16 * group + 4 * pair + x // 2], preferred_element_type=f32
                )
                for i in range(2):
                    sums = result[128 * i : 128 * i + 64] + result[128 * i + 64 : 128 * i + 128]
                    for k in range(2):
                        outs[k][pl.ds(x + i, M, stride=8), :] = sums[:, 128 * k : 128 * k + 128]
            for n in tiles:
                store(n).start()

    for n in range(count):
        store(n).wait()


def analyse(parts, order, ensemble):
    count = LX * LY * NZ // 1024
    return pl.pallas_call(
        analysis_kernel,
        in_specs=[
            pl.BlockSpec(memory_space=pltpu.VMEM),
            pl.BlockSpec(memory_space=pltpu.VMEM),
            pl.BlockSpec(memory_space=pl.ANY),
        ],
        out_specs=pl.BlockSpec(memory_space=pl.ANY),
        out_shape=jax.ShapeDtypeStruct((M, LX, LY * NZ), f32),
        scratch_shapes=[
            pltpu.VMEM((count, M, 8, 128), f32),
            pltpu.VMEM((2 * count, 256, 256), bf16),
            pltpu.VMEM((count, M, 8, 128), f32),
            pltpu.VMEM((256, 256), bf16),
            pltpu.SemaphoreType.DMA((count,)),
            pltpu.SemaphoreType.DMA((count,)),
        ],
        compiler_params=pltpu.CompilerParams(vmem_limit_bytes=40 << 20),
        name="analysis",
    )(parts, order, ensemble)


def shifted(block, shift):
    return lax.ppermute(block, "gx", [(i, (i + shift) % GX) for i in range(GX)])


def backwards(blocks, axis):
    order = [list(range(blocks.shape[0]))[::-1]]
    return lax.all_to_all(
        blocks, axis, split_axis=0, concat_axis=0, tiled=True, axis_index_groups=order
    )


def on_device(ensemble, obs_index, obs_scale, member_order):
    gx = lax.axis_index("gx")
    place = gx.astype(jnp.int32).reshape(1)
    ensemble = pltpu.with_memory_space_constraint(ensemble, pltpu.HBM)
    in_hbm = lambda table: pltpu.with_memory_space_constraint(jnp.asarray(table), pltpu.HBM)
    first_table = jnp.asarray(first_tables())
    y_table = jnp.asarray(second_table())
    cross, odd_weight, *rows = depth_modes(
        place,
        ensemble,
        in_hbm(depth_tables()),
        in_hbm(obs_index.reshape(OBS_DEV // 128, 128)),
        in_hbm(obs_scale.reshape(OBS_DEV // 128, 128)),
    )
    cross = backwards(cross, "gy")
    rows = [rows[0]] + [shifted(rows[s], s) for s in range(1, GX)]
    even = first_modes(place, first_table, rows)
    odd = second_modes(place, y_table, cross)
    even = lax.all_to_all(even, "gy", split_axis=0, concat_axis=0, tiled=True)
    odd = [odd[0]] + [shifted(odd[s], s) for s in range(1, GX)]
    parts = gram(place, first_table, y_table, odd_weight, even, odd)
    parts = backwards(parts, "gx")
    parts = jnp.broadcast_to(jnp.sum(parts, axis=0), (GY, 32, 128))
    parts = backwards(parts, "gy")
    return analyse(parts, member_order.reshape(1, M), ensemble)


def solution(mesh):
    placed = (P(None, "gx", "gy"), P(("gx", "gy")), P(("gx", "gy")), P())
    return jax.shard_map(
        on_device, mesh=mesh, in_specs=placed, out_specs=P(None, "gx", "gy"), check_vma=False
    )
```

```python
import math

import jax
import jax.numpy as jnp
import numpy as np
from jax import lax
from jax.experimental import pallas as pl
from jax.experimental.pallas import tpu as pltpu
from jax.sharding import PartitionSpec as P

M = 64
NX = 256
NY = 256
NZ = 64
XM = 64
YM = 64
ZM = 32
NS_ITERS = 18
OBS_DEV = 512
GX = 8
GY = 16
LX = NX // GX
LY = NY // GY

exact_mode = lax.Precision.HIGHEST
f32 = jnp.float32
bf16 = jnp.bfloat16


def basis(length, count):
    q = np.arange(length)
    r = np.arange(count)
    half = count // 2
    freq = np.where(r < half, r, r - half + 1)
    phase = (freq[:, None] * q[None, :] % length) * (2.0 * math.pi / length)
    scale = np.where(r == 0, math.sqrt(1.0 / length), math.sqrt(2.0 / length))
    return scale[:, None] * np.where((r < half)[:, None], np.cos(phase), np.sin(phase))


def two_parts(table, axis):
    high = table.astype(np.float32).astype(jnp.bfloat16)
    low = (table - high.astype(np.float64)).astype(np.float32).astype(jnp.bfloat16)
    return np.concatenate([high, low], axis=axis)


def depth_tables():
    bz = basis(NZ, ZM)
    out = np.zeros((GX, 128, 256))
    for g in range(GX):
        for y4 in range(4):
            cols = slice(64 * y4, 64 * y4 + 64)
            for h in range(GY):
                out[g, 16 * y4 + h, cols] = bz[2 * (GY - 1 - h) + 1]
            for s in range(GX):
                for c2 in range(2):
                    out[g, 64 + 8 * s + 2 * y4 + c2, cols] = bz[4 * ((g + s) % GX) + 2 * c2]
    return two_parts(out.transpose(0, 2, 1), 2)


def first_tables():
    bx = basis(NX, XM)
    out = np.zeros((GX, XM, GX, 2, LX // 2))
    for g in range(GX):
        for s in range(GX):
            start = LX * ((g - s) % GX)
            block = bx[:, start : start + LX]
            out[g, :, s, 0, :] = block[:, 0::2]
            out[g, :, s, 1, :] = block[:, 1::2]
    return two_parts(out.reshape(GX, XM, NX), 1)


def second_table():
    high, low = np.split(two_parts(basis(NY, YM), 0), 2)
    return np.stack([np.concatenate([part, part]) for part in (high, low)]).astype(np.float32)


def from_row(table, start):
    return jnp.concatenate([table[part, pl.ds(start, YM), :] for part in range(2)]).astype(bf16)


def split(value):
    high = value.astype(bf16)
    return high, (value - high.astype(f32)).astype(bf16)


def three_parts(value):
    high = value.astype(bf16)
    rest = value - high.astype(f32)
    middle = rest.astype(bf16)
    return high, middle, (rest - middle.astype(f32)).astype(bf16)


def contract(table, value):
    rows = table.shape[0] // 2
    high, low = split(value)
    first = jnp.dot(table, high, preferred_element_type=f32)
    second = jnp.dot(table[:rows], low, preferred_element_type=f32)
    return first[:rows] + first[rows:] + second


NT = ((1,), (1,))


SCALAR = pl.BlockSpec(memory_space=pltpu.SMEM)
WHOLE = pl.BlockSpec(memory_space=pltpu.VMEM)


def half_lanes(shape):
    return lax.broadcasted_iota(jnp.int32, shape, 1) < 64


def unpair(one, two):
    left = half_lanes(one.shape)
    return jnp.concatenate(
        [
            jnp.where(left, one, pltpu.roll(two, 64, 1)),
            jnp.where(left, pltpu.roll(one, 64, 1), two),
        ]
    )


def mode_weights(index, scale):
    square = scale * (1.0 / math.sqrt(M - 1))
    square = square * square
    high = lax.broadcasted_iota(jnp.int32, (16, OBS_DEV), 0) == (index >> 6)
    low = lax.broadcasted_iota(jnp.int32, (XM, OBS_DEV), 0) == (index & 63)
    parts = jnp.concatenate(
        [jnp.where(high, part.astype(f32), 0.0) for part in three_parts(square)]
    ).astype(bf16)
    sums = lax.dot_general(
        parts, low.astype(f32).astype(bf16), (NT, ((), ())), preferred_element_type=f32
    )
    return sums[:16] + sums[16:32] + sums[32:]


def one_row(ref):
    return jnp.concatenate([ref[i : i + 1, :] for i in range(OBS_DEV // 128)], axis=1)


def depth_kernel(place, ens, table_ref, index, scale, cross_ref, odd_weight, *refs):
    del place
    row_refs, held = refs[:GX], refs[GX]
    step = pl.program_id(0)

    @pl.when(step == 0)
    def _():
        weight = mode_weights(one_row(index), one_row(scale))
        weight = jnp.concatenate([weight, jnp.zeros((16, 64), f32)], axis=1)
        odd_weight[...] = weight[8:]
        for ref in row_refs:
            ref[512:520, :] = weight[:8]

    cross = cross_ref.reshape(GY * 4 * LY, 128)
    table = table_ref[0]
    for quad in range(4):
        lanes = slice(256 * quad, 256 * quad + 256)
        block = ens[:, :, lanes]
        block = (block - jnp.sum(block, axis=0, keepdims=True) * (1.0 / M)).reshape(M * 8, 256)
        high, low = split(block)
        first = jnp.dot(high, table, preferred_element_type=f32)
        second = jnp.dot(low, table[:, :128], preferred_element_type=f32)
        held[quad] = first[:, :128] + first[:, 128:] + second
        for p in range(4):
            modes = jnp.concatenate(
                [held[quad, pl.ds(2 * p + parity, M, stride=8), :] for parity in range(2)]
            ).T
            for y4 in range(4):
                cross[pl.ds(LY * p + 4 * quad + y4, GY, stride=4 * LY), :] = modes[
                    16 * y4 : 16 * y4 + 16
                ]
            for shift in range(GX):
                start = pl.multiple_of(128 * step + 32 * p + 8 * quad, 8)
                row_refs[shift][pl.ds(start, 8), :] = modes[64 + 8 * shift : 72 + 8 * shift]


def depth_modes(place, ensemble, tables, index, scale):
    grid_spec = pltpu.PrefetchScalarGridSpec(
        num_scalar_prefetch=1,
        grid=(LX // 8,),
        in_specs=[pl.BlockSpec((M, 8, LY * NZ), lambda i, place: (0, i, 0))]
        + [pl.BlockSpec((1, 256, 256), lambda i, place: (place[0], 0, 0))]
        + [pl.BlockSpec((OBS_DEV // 128, 128), lambda i, place: (0, 0))] * 2,
        out_specs=[
            pl.BlockSpec((GY, 4, LY, 128), lambda i, place: (0, i, 0, 0)),
            pl.BlockSpec((8, 128), lambda i, place: (0, 0)),
        ]
        + [pl.BlockSpec((520, 128), lambda i, place: (0, 0))] * GX,
        scratch_shapes=[pltpu.VMEM((4, M * 8, 128), f32)],
    )
    return pl.pallas_call(
        depth_kernel,
        grid_spec=grid_spec,
        out_shape=[pltpu.HBM((GY, LX // 2, LY, 128), f32)]
        + [jax.ShapeDtypeStruct(shape, f32) for shape in ((8, 128), (520, 128))]
        + [pltpu.HBM((520, 128), f32)] * (GX - 1),
        compiler_params=pltpu.CompilerParams(vmem_limit_bytes=48 << 20),
        name="depth_modes",
    )(place, ensemble, tables, index, scale)


def first_product(blocks, columns, table, y):
    value = [
        jnp.concatenate(
            [unpair(*[b[pl.ds(2 * k + c2, 16, stride=32), :] for c2 in range(2)]) for b in blocks]
        )
        for k in (y, y + 1)
    ]
    return contract(table[:, columns], jnp.concatenate(value, axis=1))


def first_half_kernel(place, table_ref, *refs):
    blocks, out = refs[: GX // 2], refs[GX // 2]
    table = table_ref[place[0]]
    for y in range(0, LY, 2):
        out[y // 2] = first_product(blocks, slice(0, NX // 2), table, y)


def first_kernel(place, table_ref, half, *refs):
    blocks, out_ref, held = refs[:GX], refs[GX], refs[GX + 1]
    out = out_ref.reshape(XM * 18, 128)
    held[64:, :] = jnp.zeros((64, 128), f32)
    for shift in range(GX):
        start = pl.multiple_of(8 * ((place[0] + GX - shift) % GX), 8)
        held[pl.ds(start, 8), :] = blocks[shift][512:520, :]
    out[pl.ds(16, XM, stride=18), :] = held[...].T[:64]
    out[pl.ds(17, XM, stride=18), :] = jnp.zeros((XM, 128), f32)
    table = table_ref[place[0]]
    for y in range(0, LY, 2):
        modes = half[y // 2] + first_product(blocks[GX // 2 :], slice(NX // 2, NX), table, y)
        for k in range(2):
            out[pl.ds(y + k, XM, stride=18), :] = modes[:, 128 * k : 128 * k + 128]


def first_modes(place, tables, blocks):
    params = pltpu.CompilerParams(vmem_limit_bytes=16 << 20)
    half = pl.pallas_call(
        first_half_kernel,
        in_specs=[SCALAR] + [WHOLE] * (GX // 2 + 1),
        out_specs=WHOLE,
        out_shape=jax.ShapeDtypeStruct((LY // 2, XM, 256), f32),
        compiler_params=params,
        name="first_half",
    )(place, tables, *blocks[: GX // 2])
    return pl.pallas_call(
        first_kernel,
        in_specs=[SCALAR] + [WHOLE] * (GX + 2),
        out_specs=WHOLE,
        out_shape=pltpu.HBM((GY, 72, 128), f32),
        scratch_shapes=[pltpu.VMEM((128, 128), f32)],
        compiler_params=params,
        name="first_modes",
    )(place, tables, half, *blocks)


def second_kernel(place, table_ref, cross, *outs):
    table = from_row(table_ref, pl.multiple_of(8 * place[0], 8))
    for group in range(LX // 4):
        value = jnp.concatenate(
            [
                jnp.concatenate([cross[h, 2 * group + pair] for h in reversed(range(GY))])
                for pair in range(2)
            ],
            axis=1,
        )
        modes = contract(table, value)
        for pair in range(2):
            for shift in range(GX):
                outs[shift].reshape(128, 128)[
                    pl.ds(2 * group + pair, 8, stride=16), :
                ] = modes[8 * shift : 8 * shift + 8, 128 * pair : 128 * pair + 128]


def second_modes(place, tables, cross):
    return pl.pallas_call(
        second_kernel,
        in_specs=[SCALAR, WHOLE, WHOLE],
        out_specs=[WHOLE] * GX,
        out_shape=[jax.ShapeDtypeStruct((8, 16, 128), f32)]
        + [pltpu.HBM((8, 16, 128), f32)] * (GX - 1),
        compiler_params=pltpu.CompilerParams(vmem_limit_bytes=16 << 20),
        name="second_modes",
    )(place, tables, cross)


def pack(gram):
    group = lax.broadcasted_iota(jnp.int32, (8, 128), 1) // 32
    corner = jnp.zeros((8, 128), f32)
    for i in range(4):
        rows = gram[32 + 8 * i : 40 + 8 * i]
        corner = jnp.where(group == i, pltpu.roll(rows, (32 * i - 32) % 128, 1), corner)
    upper = jnp.where(half_lanes((16, 128)), gram[:16], pltpu.roll(gram[16:32], 64, 1))
    return jnp.concatenate([upper, corner])


def unpack(packed):
    upper, corner = packed[:16], packed[16:]
    lower = jnp.concatenate([pltpu.roll(corner, (32 - 32 * i) % 128, 1) for i in range(4)])
    half = jnp.concatenate([upper[:, :64], pltpu.roll(upper, 64, 1)[:, :64], lower[:, :64]])
    row = lax.broadcasted_iota(jnp.int32, (M, M), 0)
    column = lax.broadcasted_iota(jnp.int32, (M, M), 1)
    return jnp.where((row >= 32) & (column < 32), half.T, half)


def gram_kernel(place, first_table, table_ref, odd_weight, even_ref, *refs):
    odd_refs, out = refs[:GX], refs[GX]
    total = jnp.zeros((128, 128), f32)

    def add(rows, one, two):
        top = lax.broadcasted_iota(jnp.int32, (128, 256), 0) < 64
        weight = jnp.where(top, jnp.concatenate(one, axis=1), jnp.concatenate(two, axis=1))
        return jnp.dot(
            rows.T * weight, rows, precision=exact_mode, preferred_element_type=f32
        )

    table = from_row(table_ref, 0)
    rows = []
    for pair in range(2):
        value = jnp.concatenate(
            [
                jnp.concatenate([even_ref[h, 18 * a : 18 * a + 16] for h in range(GY)])
                for a in (2 * pair, 2 * pair + 1)
            ],
            axis=1,
        )
        modes = contract(table, value)
        rows += [modes[:, :128], modes[:, 128:]]
    weights = [
        [even_ref[2 * place[0] + c2, 18 * a + 16 : 18 * a + 17, :64] for a in range(4)]
        for c2 in range(2)
    ]
    total += add(jnp.concatenate(rows), *weights)
    table = first_table[place[0]]
    rows = []
    for b in range(0, 8, 4):
        value = [
            jnp.concatenate([unpair(*[ref[k + b2] for b2 in range(2)]) for ref in odd_refs])
            for k in (b, b + 2)
        ]
        modes = contract(table, jnp.concatenate(value, axis=1))
        rows += [modes[:, :128], modes[:, 128:]]
    weights = [[odd_weight[b : b + 1, :64] for b in range(b2, 8, 2)] for b2 in range(2)]
    total += add(jnp.concatenate(rows), *weights)
    gram = total[:64] + pltpu.roll(total[64:], 64, 1)
    packed = pack(gram)
    for i in range(GX):
        out[i] = packed


def gram(place, first_table, second_table, odd_weight, even, odd):
    return pl.pallas_call(
        gram_kernel,
        in_specs=[SCALAR] + [WHOLE] * (GX + 4),
        out_specs=WHOLE,
        out_shape=jax.ShapeDtypeStruct((GX, 24, 128), f32),
        compiler_params=pltpu.CompilerParams(vmem_limit_bytes=16 << 20),
        name="gram",
    )(place, first_table, second_table, odd_weight, even, *odd)


def exact_dot(one, two):
    a, b, c = three_parts(one)
    d, e, f = three_parts(two)
    first = jnp.dot(jnp.concatenate([a, b, c]), d, preferred_element_type=f32)
    second = jnp.dot(jnp.concatenate([a, b]), e, preferred_element_type=f32)
    third = jnp.dot(a, f, preferred_element_type=f32)
    return first[:M] + (second[:M] + first[M : 2 * M]) + (first[2 * M :] + second[M:] + third)


def combine_table(parts, order, beside):
    packed = jnp.sum(parts, axis=0)
    row = lax.broadcasted_iota(jnp.int32, (M, M), 0)
    column = lax.broadcasted_iota(jnp.int32, (M, M), 1)
    identity = (row == column).astype(f32)
    matrix = identity + unpack(packed)
    squares = jnp.sum(jnp.sum(matrix * matrix, axis=1, keepdims=True), axis=0, keepdims=True)
    frobenius = jnp.sqrt(squares)

    def sweep(turn, carry):
        root, inverse = carry
        change = 1.5 * identity - 0.5 * exact_dot(inverse, root)
        return exact_dot(root, change), exact_dot(change, inverse)

    def sweep_beside(turn, carry):
        beside(turn)
        return sweep(turn, carry)

    carry = lax.fori_loop(0, 16, sweep_beside, (matrix / frobenius, identity))
    _, inverse = lax.fori_loop(16, NS_ITERS, sweep, carry)
    transform = inverse / jnp.sqrt(frobenius)
    chosen = (order == row).astype(f32).T
    weight = lax.dot_general(
        chosen, transform, (NT, ((), ())), precision=exact_mode, preferred_element_type=f32
    )
    high, low = split(weight)
    high, low = high.astype(f32), low.astype(f32)
    none = jnp.zeros((M, M), f32)
    return jnp.concatenate(
        [
            jnp.concatenate([high, high, none, none], axis=1),
            jnp.concatenate([low, none, none, none], axis=1),
            jnp.concatenate([none, none, high, high], axis=1),
            jnp.concatenate([none, none, low, none], axis=1),
        ]
    ).astype(bf16)


def analysis_kernel(parts, order, ens_hbm, out_hbm, ens, ready, out, weights, fetched, stored):
    def fetch(n):
        i, t = n // 8, n % 8
        place = (slice(None), pl.ds(8 * i, 8), pl.ds(128 * t, 128))
        return pltpu.make_async_copy(ens_hbm.at[place], ens.at[n], fetched.at[n])

    def store(n):
        i, t = n // 8, n % 8
        place = (slice(None), pl.ds(8 * i, 8), pl.ds(128 * t, 128))
        return pltpu.make_async_copy(out.at[n], out_hbm.at[place], stored.at[n])

    count = LX * LY * NZ // 1024
    for n in range(count):
        fetch(n).start()

    def prepare(pair):
        tiles = (2 * pair, 2 * pair + 1)
        for n in tiles:
            fetch(n).wait()
        means = [jnp.sum(ens[n], axis=0) * (1.0 / M) for n in tiles]
        flats = [ens.at[n].reshape(M * 8, 128) for n in tiles]
        for x in range(8):
            high, low = split(
                jnp.concatenate(
                    [flats[k][pl.ds(x, M, stride=8), :] - means[k][x : x + 1] for k in range(2)],
                    axis=1,
                )
            )
            ready[4 * pair + x // 2, 128 * (x % 2) : 128 * (x % 2) + 64] = high
            ready[4 * pair + x // 2, 128 * (x % 2) + 64 : 128 * (x % 2) + 128] = low

    weights[...] = combine_table(parts[...], order[...], prepare)

    @pl.loop(0, LX // 8)
    def _(group):
        table = weights[...]
        for pair in range(4):
            tiles = (8 * group + 2 * pair, 8 * group + 2 * pair + 1)
            outs = [out.at[n].reshape(M * 8, 128) for n in tiles]
            for x in range(0, 8, 2):
                result = jnp.dot(
                    table, ready[16 * group + 4 * pair + x // 2], preferred_element_type=f32
                )
                for i in range(2):
                    sums = result[128 * i : 128 * i + 64] + result[128 * i + 64 : 128 * i + 128]
                    for k in range(2):
                        outs[k][pl.ds(x + i, M, stride=8), :] = sums[:, 128 * k : 128 * k + 128]
            for n in tiles:
                store(n).start()

    for n in range(count):
        store(n).wait()


def analyse(parts, order, ensemble):
    count = LX * LY * NZ // 1024
    return pl.pallas_call(
        analysis_kernel,
        in_specs=[
            pl.BlockSpec(memory_space=pltpu.VMEM),
            pl.BlockSpec(memory_space=pltpu.VMEM),
            pl.BlockSpec(memory_space=pl.ANY),
        ],
        out_specs=pl.BlockSpec(memory_space=pl.ANY),
        out_shape=jax.ShapeDtypeStruct((M, LX, LY * NZ), f32),
        scratch_shapes=[
            pltpu.VMEM((count, M, 8, 128), f32),
            pltpu.VMEM((2 * count, 256, 256), bf16),
            pltpu.VMEM((count, M, 8, 128), f32),
            pltpu.VMEM((256, 256), bf16),
            pltpu.SemaphoreType.DMA((count,)),
            pltpu.SemaphoreType.DMA((count,)),
        ],
        compiler_params=pltpu.CompilerParams(vmem_limit_bytes=40 << 20),
        name="analysis",
    )(parts, order, ensemble)


def shifted(block, shift):
    return lax.ppermute(block, "gx", [(i, (i + shift) % GX) for i in range(GX)])


def backwards(blocks, axis):
    order = [list(range(blocks.shape[0]))[::-1]]
    return lax.all_to_all(
        blocks, axis, split_axis=0, concat_axis=0, tiled=True, axis_index_groups=order
    )


def on_device(ensemble, obs_index, obs_scale, member_order):
    gx = lax.axis_index("gx")
    place = gx.astype(jnp.int32).reshape(1)
    ensemble = pltpu.with_memory_space_constraint(ensemble, pltpu.HBM)
    in_hbm = lambda table: pltpu.with_memory_space_constraint(jnp.asarray(table), pltpu.HBM)
    first_table = jnp.asarray(first_tables())
    y_table = jnp.asarray(second_table())
    cross, odd_weight, *rows = depth_modes(
        place,
        ensemble,
        in_hbm(depth_tables()),
        in_hbm(obs_index.reshape(OBS_DEV // 128, 128)),
        in_hbm(obs_scale.reshape(OBS_DEV // 128, 128)),
    )
    cross = backwards(cross, "gy")
    rows = [rows[0]] + [shifted(rows[s], s) for s in range(1, GX)]
    even = first_modes(place, first_table, rows)
    odd = second_modes(place, y_table, cross)
    even = lax.all_to_all(even, "gy", split_axis=0, concat_axis=0, tiled=True)
    odd = [odd[0]] + [shifted(odd[s], s) for s in range(1, GX)]
    parts = gram(place, first_table, y_table, odd_weight, even, odd)
    parts = backwards(parts, "gx")
    parts = jnp.broadcast_to(jnp.sum(parts, axis=0), (GY, 24, 128))
    parts = backwards(parts, "gy")
    return analyse(parts, member_order.reshape(1, M), ensemble)


def solution(mesh):
    placed = (P(None, "gx", "gy"), P(("gx", "gy")), P(("gx", "gy")), P())
    return jax.shard_map(
        on_device, mesh=mesh, in_specs=placed, out_specs=P(None, "gx", "gy"), check_vma=False
    )
```

```python
import math

import jax
import jax.numpy as jnp
import numpy as np
from jax import lax
from jax.experimental import pallas as pl
from jax.experimental.pallas import tpu as pltpu
from jax.sharding import PartitionSpec as P

M = 64
NX = 256
NY = 256
NZ = 64
XM = 64
YM = 64
ZM = 32
NS_ITERS = 18
OBS_DEV = 512
GX = 8
GY = 16
LX = NX // GX
LY = NY // GY

exact_mode = lax.Precision.HIGHEST
f32 = jnp.float32
bf16 = jnp.bfloat16


def basis(length, count):
    q = np.arange(length)
    r = np.arange(count)
    half = count // 2
    freq = np.where(r < half, r, r - half + 1)
    phase = (freq[:, None] * q[None, :] % length) * (2.0 * math.pi / length)
    scale = np.where(r == 0, math.sqrt(1.0 / length), math.sqrt(2.0 / length))
    return scale[:, None] * np.where((r < half)[:, None], np.cos(phase), np.sin(phase))


def two_parts(table, axis):
    high = table.astype(np.float32).astype(jnp.bfloat16)
    low = (table - high.astype(np.float64)).astype(np.float32).astype(jnp.bfloat16)
    return np.concatenate([high, low], axis=axis)


def depth_tables():
    bz = basis(NZ, ZM)
    out = np.zeros((GX, 128, 256))
    for g in range(GX):
        for y4 in range(4):
            cols = slice(64 * y4, 64 * y4 + 64)
            for h in range(GY):
                out[g, 16 * y4 + h, cols] = bz[2 * (GY - 1 - h) + 1]
            for s in range(GX):
                for c2 in range(2):
                    out[g, 64 + 8 * s + 2 * y4 + c2, cols] = bz[4 * ((g + s) % GX) + 2 * c2]
    return two_parts(out.transpose(0, 2, 1), 2)


def first_tables():
    bx = basis(NX, XM)
    out = np.zeros((GX, XM, GX, 2, LX // 2))
    for g in range(GX):
        for s in range(GX):
            start = LX * ((g - s) % GX)
            block = bx[:, start : start + LX]
            out[g, :, s, 0, :] = block[:, 0::2]
            out[g, :, s, 1, :] = block[:, 1::2]
    return two_parts(out.reshape(GX, XM, NX), 1)


def second_table():
    high, low = np.split(two_parts(basis(NY, YM), 0), 2)
    return np.stack([np.concatenate([part, part]) for part in (high, low)]).astype(np.float32)


def from_row(table, start):
    return jnp.concatenate([table[part, pl.ds(start, YM), :] for part in range(2)]).astype(bf16)


def split(value):
    high = value.astype(bf16)
    return high, (value - high.astype(f32)).astype(bf16)


def three_parts(value):
    high = value.astype(bf16)
    rest = value - high.astype(f32)
    middle = rest.astype(bf16)
    return high, middle, (rest - middle.astype(f32)).astype(bf16)


def contract(table, value):
    rows = table.shape[0] // 2
    high, low = split(value)
    first = jnp.dot(table, high, preferred_element_type=f32)
    second = jnp.dot(table[:rows], low, preferred_element_type=f32)
    return first[:rows] + first[rows:] + second


NT = ((1,), (1,))


SCALAR = pl.BlockSpec(memory_space=pltpu.SMEM)
WHOLE = pl.BlockSpec(memory_space=pltpu.VMEM)


def half_lanes(shape):
    return lax.broadcasted_iota(jnp.int32, shape, 1) < 64


def unpair(one, two):
    left = half_lanes(one.shape)
    return jnp.concatenate(
        [
            jnp.where(left, one, pltpu.roll(two, 64, 1)),
            jnp.where(left, pltpu.roll(one, 64, 1), two),
        ]
    )


def mode_weights(index, scale):
    square = scale * (1.0 / math.sqrt(M - 1))
    square = square * square
    high = lax.broadcasted_iota(jnp.int32, (16, OBS_DEV), 0) == (index >> 6)
    low = lax.broadcasted_iota(jnp.int32, (XM, OBS_DEV), 0) == (index & 63)
    parts = jnp.concatenate(
        [jnp.where(high, part.astype(f32), 0.0) for part in three_parts(square)]
    ).astype(bf16)
    sums = lax.dot_general(
        parts, low.astype(f32).astype(bf16), (NT, ((), ())), preferred_element_type=f32
    )
    return sums[:16] + sums[16:32] + sums[32:]


def one_row(ref):
    return jnp.concatenate([ref[i : i + 1, :] for i in range(OBS_DEV // 128)], axis=1)


def depth_kernel(place, ens, table_ref, index, scale, cross_ref, odd_weight, *refs):
    del place
    row_refs, held = refs[:GX], refs[GX]
    step = pl.program_id(0)

    @pl.when(step == 0)
    def _():
        weight = mode_weights(one_row(index), one_row(scale))
        weight = jnp.concatenate([weight, jnp.zeros((16, 64), f32)], axis=1)
        odd_weight[...] = weight[8:]
        for ref in row_refs:
            ref[512:520, :] = weight[:8]

    cross = cross_ref.reshape(GY * 4 * LY, 128)
    table = table_ref[0]
    for quad in range(4):
        lanes = slice(256 * quad, 256 * quad + 256)
        block = ens[:, :, lanes]
        block = (block - jnp.sum(block, axis=0, keepdims=True) * (1.0 / M)).reshape(M * 8, 256)
        high, low = split(block)
        first = jnp.dot(high, table, preferred_element_type=f32)
        second = jnp.dot(low, table[:, :128], preferred_element_type=f32)
        held[quad] = first[:, :128] + first[:, 128:] + second
        for p in range(4):
            modes = jnp.concatenate(
                [held[quad, pl.ds(2 * p + parity, M, stride=8), :] for parity in range(2)]
            ).T
            for y4 in range(4):
                cross[pl.ds(LY * p + 4 * quad + y4, GY, stride=4 * LY), :] = modes[
                    16 * y4 : 16 * y4 + 16
                ]
            for shift in range(GX):
                start = pl.multiple_of(128 * step + 32 * p + 8 * quad, 8)
                row_refs[shift][pl.ds(start, 8), :] = modes[64 + 8 * shift : 72 + 8 * shift]


def depth_modes(place, ensemble, tables, index, scale):
    grid_spec = pltpu.PrefetchScalarGridSpec(
        num_scalar_prefetch=1,
        grid=(LX // 8,),
        in_specs=[pl.BlockSpec((M, 8, LY * NZ), lambda i, place: (0, i, 0))]
        + [pl.BlockSpec((1, 256, 256), lambda i, place: (place[0], 0, 0))]
        + [pl.BlockSpec((OBS_DEV // 128, 128), lambda i, place: (0, 0))] * 2,
        out_specs=[
            pl.BlockSpec((GY, 4, LY, 128), lambda i, place: (0, i, 0, 0)),
            pl.BlockSpec((8, 128), lambda i, place: (0, 0)),
        ]
        + [pl.BlockSpec((520, 128), lambda i, place: (0, 0))] * GX,
        scratch_shapes=[pltpu.VMEM((4, M * 8, 128), f32)],
    )
    return pl.pallas_call(
        depth_kernel,
        grid_spec=grid_spec,
        out_shape=[pltpu.HBM((GY, LX // 2, LY, 128), f32)]
        + [jax.ShapeDtypeStruct(shape, f32) for shape in ((8, 128), (520, 128))]
        + [pltpu.HBM((520, 128), f32)] * (GX - 1),
        compiler_params=pltpu.CompilerParams(vmem_limit_bytes=48 << 20),
        name="depth_modes",
    )(place, ensemble, tables, index, scale)


def first_product(blocks, columns, table, y):
    value = [
        jnp.concatenate(
            [unpair(*[b[pl.ds(2 * k + c2, 16, stride=32), :] for c2 in range(2)]) for b in blocks]
        )
        for k in (y, y + 1)
    ]
    return contract(table[:, columns], jnp.concatenate(value, axis=1))


def first_half_kernel(place, table_ref, *refs):
    blocks, out = refs[: GX // 2], refs[GX // 2]
    table = table_ref[place[0]]
    for y in range(0, LY, 2):
        out[y // 2] = first_product(blocks, slice(0, NX // 2), table, y)


def first_kernel(place, table_ref, half, *refs):
    blocks, out_ref, held = refs[:GX], refs[GX], refs[GX + 1]
    out = out_ref.reshape(XM * 18, 128)
    held[64:, :] = jnp.zeros((64, 128), f32)
    for shift in range(GX):
        start = pl.multiple_of(8 * ((place[0] + GX - shift) % GX), 8)
        held[pl.ds(start, 8), :] = blocks[shift][512:520, :]
    out[pl.ds(16, XM, stride=18), :] = held[...].T[:64]
    out[pl.ds(17, XM, stride=18), :] = jnp.zeros((XM, 128), f32)
    table = table_ref[place[0]]
    for y in range(0, LY, 2):
        modes = half[y // 2] + first_product(blocks[GX // 2 :], slice(NX // 2, NX), table, y)
        for k in range(2):
            out[pl.ds(y + k, XM, stride=18), :] = modes[:, 128 * k : 128 * k + 128]


def first_modes(place, tables, blocks):
    params = pltpu.CompilerParams(vmem_limit_bytes=16 << 20)
    half = pl.pallas_call(
        first_half_kernel,
        in_specs=[SCALAR] + [WHOLE] * (GX // 2 + 1),
        out_specs=WHOLE,
        out_shape=jax.ShapeDtypeStruct((LY // 2, XM, 256), f32),
        compiler_params=params,
        name="first_half",
    )(place, tables, *blocks[: GX // 2])
    return pl.pallas_call(
        first_kernel,
        in_specs=[SCALAR] + [WHOLE] * (GX + 2),
        out_specs=WHOLE,
        out_shape=pltpu.HBM((GY, 72, 128), f32),
        scratch_shapes=[pltpu.VMEM((128, 128), f32)],
        compiler_params=params,
        name="first_modes",
    )(place, tables, half, *blocks)


def second_kernel(place, table_ref, cross, *outs):
    table = from_row(table_ref, pl.multiple_of(8 * place[0], 8))
    for group in range(LX // 4):
        value = jnp.concatenate(
            [
                jnp.concatenate([cross[h, 2 * group + pair] for h in reversed(range(GY))])
                for pair in range(2)
            ],
            axis=1,
        )
        modes = contract(table, value)
        for pair in range(2):
            for shift in range(GX):
                outs[shift].reshape(128, 128)[
                    pl.ds(2 * group + pair, 8, stride=16), :
                ] = modes[8 * shift : 8 * shift + 8, 128 * pair : 128 * pair + 128]


def second_modes(place, tables, cross):
    return pl.pallas_call(
        second_kernel,
        in_specs=[SCALAR, WHOLE, WHOLE],
        out_specs=[WHOLE] * GX,
        out_shape=[jax.ShapeDtypeStruct((8, 16, 128), f32)]
        + [pltpu.HBM((8, 16, 128), f32)] * (GX - 1),
        compiler_params=pltpu.CompilerParams(vmem_limit_bytes=16 << 20),
        name="second_modes",
    )(place, tables, cross)


def pack(gram):
    group = lax.broadcasted_iota(jnp.int32, (8, 128), 1) // 32
    corner = jnp.zeros((8, 128), f32)
    for i in range(4):
        rows = gram[32 + 8 * i : 40 + 8 * i]
        corner = jnp.where(group == i, pltpu.roll(rows, (32 * i - 32) % 128, 1), corner)
    upper = jnp.where(half_lanes((16, 128)), gram[:16], pltpu.roll(gram[16:32], 64, 1))
    return jnp.concatenate([upper, corner])


def unpack(packed):
    upper, corner = packed[:16], packed[16:]
    lower = jnp.concatenate([pltpu.roll(corner, (32 - 32 * i) % 128, 1) for i in range(4)])
    half = jnp.concatenate([upper[:, :64], pltpu.roll(upper, 64, 1)[:, :64], lower[:, :64]])
    row = lax.broadcasted_iota(jnp.int32, (M, M), 0)
    column = lax.broadcasted_iota(jnp.int32, (M, M), 1)
    return jnp.where((row >= 32) & (column < 32), half.T, half)


def gram_kernel(place, first_table, table_ref, odd_weight, even_ref, *refs):
    odd_refs, out = refs[:GX], refs[GX]
    total = jnp.zeros((128, 128), f32)

    def add(rows, one, two):
        top = lax.broadcasted_iota(jnp.int32, (128, 256), 0) < 64
        weight = jnp.where(top, jnp.concatenate(one, axis=1), jnp.concatenate(two, axis=1))
        return jnp.dot(
            rows.T * weight, rows, precision=exact_mode, preferred_element_type=f32
        )

    table = from_row(table_ref, 0)
    rows = []
    for pair in range(2):
        value = jnp.concatenate(
            [
                jnp.concatenate([even_ref[h, 18 * a : 18 * a + 16] for h in range(GY)])
                for a in (2 * pair, 2 * pair + 1)
            ],
            axis=1,
        )
        modes = contract(table, value)
        rows += [modes[:, :128], modes[:, 128:]]
    weights = [
        [even_ref[2 * place[0] + c2, 18 * a + 16 : 18 * a + 17, :64] for a in range(4)]
        for c2 in range(2)
    ]
    total += add(jnp.concatenate(rows), *weights)
    table = first_table[place[0]]
    rows = []
    for b in range(0, 8, 4):
        value = [
            jnp.concatenate([unpair(*[ref[k + b2] for b2 in range(2)]) for ref in odd_refs])
            for k in (b, b + 2)
        ]
        modes = contract(table, jnp.concatenate(value, axis=1))
        rows += [modes[:, :128], modes[:, 128:]]
    weights = [[odd_weight[b : b + 1, :64] for b in range(b2, 8, 2)] for b2 in range(2)]
    total += add(jnp.concatenate(rows), *weights)
    gram = total[:64] + pltpu.roll(total[64:], 64, 1)
    packed = pack(gram)
    for i in range(GX):
        out[i] = packed


def gram(place, first_table, second_table, odd_weight, even, odd):
    return pl.pallas_call(
        gram_kernel,
        in_specs=[SCALAR] + [WHOLE] * (GX + 4),
        out_specs=WHOLE,
        out_shape=jax.ShapeDtypeStruct((GX, 24, 128), f32),
        compiler_params=pltpu.CompilerParams(vmem_limit_bytes=16 << 20),
        name="gram",
    )(place, first_table, second_table, odd_weight, even, *odd)


def exact_dot(one, two):
    a, b, c = three_parts(one)
    d, e, f = three_parts(two)
    first = jnp.dot(jnp.concatenate([a, b, c]), d, preferred_element_type=f32)
    second = jnp.dot(jnp.concatenate([a, b]), e, preferred_element_type=f32)
    third = jnp.dot(a, f, preferred_element_type=f32)
    return first[:M] + (second[:M] + first[M : 2 * M]) + (first[2 * M :] + second[M:] + third)


def combine_table(parts, order, beside):
    packed = jnp.sum(parts, axis=0)
    row = lax.broadcasted_iota(jnp.int32, (M, M), 0)
    column = lax.broadcasted_iota(jnp.int32, (M, M), 1)
    identity = (row == column).astype(f32)
    matrix = identity + unpack(packed)
    squares = jnp.sum(jnp.sum(matrix * matrix, axis=1, keepdims=True), axis=0, keepdims=True)
    frobenius = jnp.sqrt(squares)

    def sweep(turn, carry):
        root, inverse = carry
        change = 1.5 * identity + exact_dot(inverse, root)
        return exact_dot(root, change), exact_dot(change, inverse)

    def sweep_beside(turn, carry):
        beside(turn)
        return sweep(turn, carry)

    carry = lax.fori_loop(0, 16, sweep_beside, (-0.5 * (matrix / frobenius), identity))
    _, inverse = lax.fori_loop(16, NS_ITERS, sweep, carry)
    transform = inverse / jnp.sqrt(frobenius)
    chosen = (order == row).astype(f32).T
    weight = lax.dot_general(
        chosen, transform, (NT, ((), ())), precision=exact_mode, preferred_element_type=f32
    )
    high, low = split(weight)
    high, low = high.astype(f32), low.astype(f32)
    none = jnp.zeros((M, M), f32)
    return jnp.concatenate(
        [
            jnp.concatenate([high, high, none, none], axis=1),
            jnp.concatenate([low, none, none, none], axis=1),
            jnp.concatenate([none, none, high, high], axis=1),
            jnp.concatenate([none, none, low, none], axis=1),
        ]
    ).astype(bf16)


def analysis_kernel(parts, order, ens_hbm, out_hbm, ens, ready, out, weights, fetched, stored):
    def fetch(n):
        i, t = n // 8, n % 8
        place = (slice(None), pl.ds(8 * i, 8), pl.ds(128 * t, 128))
        return pltpu.make_async_copy(ens_hbm.at[place], ens.at[n], fetched.at[n])

    def store(n):
        i, t = n // 8, n % 8
        place = (slice(None), pl.ds(8 * i, 8), pl.ds(128 * t, 128))
        return pltpu.make_async_copy(out.at[n], out_hbm.at[place], stored.at[n])

    count = LX * LY * NZ // 1024
    for n in range(count):
        fetch(n).start()

    def prepare(pair):
        tiles = (2 * pair, 2 * pair + 1)
        for n in tiles:
            fetch(n).wait()
        means = [jnp.sum(ens[n], axis=0) * (1.0 / M) for n in tiles]
        flats = [ens.at[n].reshape(M * 8, 128) for n in tiles]
        for x in range(8):
            high, low = split(
                jnp.concatenate(
                    [flats[k][pl.ds(x, M, stride=8), :] - means[k][x : x + 1] for k in range(2)],
                    axis=1,
                )
            )
            ready[4 * pair + x // 2, 128 * (x % 2) : 128 * (x % 2) + 64] = high
            ready[4 * pair + x // 2, 128 * (x % 2) + 64 : 128 * (x % 2) + 128] = low

    weights[...] = combine_table(parts[...], order[...], prepare)

    @pl.loop(0, LX // 8)
    def _(group):
        table = weights[...]
        for pair in range(4):
            tiles = (8 * group + 2 * pair, 8 * group + 2 * pair + 1)
            outs = [out.at[n].reshape(M * 8, 128) for n in tiles]
            for x in range(0, 8, 2):
                result = jnp.dot(
                    table, ready[16 * group + 4 * pair + x // 2], preferred_element_type=f32
                )
                for i in range(2):
                    sums = result[128 * i : 128 * i + 64] + result[128 * i + 64 : 128 * i + 128]
                    for k in range(2):
                        outs[k][pl.ds(x + i, M, stride=8), :] = sums[:, 128 * k : 128 * k + 128]
            for n in tiles:
                store(n).start()

    for n in range(count):
        store(n).wait()


def analyse(parts, order, ensemble):
    count = LX * LY * NZ // 1024
    return pl.pallas_call(
        analysis_kernel,
        in_specs=[
            pl.BlockSpec(memory_space=pltpu.VMEM),
            pl.BlockSpec(memory_space=pltpu.VMEM),
            pl.BlockSpec(memory_space=pl.ANY),
        ],
        out_specs=pl.BlockSpec(memory_space=pl.ANY),
        out_shape=jax.ShapeDtypeStruct((M, LX, LY * NZ), f32),
        scratch_shapes=[
            pltpu.VMEM((count, M, 8, 128), f32),
            pltpu.VMEM((2 * count, 256, 256), bf16),
            pltpu.VMEM((count, M, 8, 128), f32),
            pltpu.VMEM((256, 256), bf16),
            pltpu.SemaphoreType.DMA((count,)),
            pltpu.SemaphoreType.DMA((count,)),
        ],
        compiler_params=pltpu.CompilerParams(vmem_limit_bytes=40 << 20),
        name="analysis",
    )(parts, order, ensemble)


def shifted(block, shift):
    return lax.ppermute(block, "gx", [(i, (i + shift) % GX) for i in range(GX)])


def backwards(blocks, axis):
    order = [list(range(blocks.shape[0]))[::-1]]
    return lax.all_to_all(
        blocks, axis, split_axis=0, concat_axis=0, tiled=True, axis_index_groups=order
    )


def on_device(ensemble, obs_index, obs_scale, member_order):
    gx = lax.axis_index("gx")
    place = gx.astype(jnp.int32).reshape(1)
    ensemble = pltpu.with_memory_space_constraint(ensemble, pltpu.HBM)
    in_hbm = lambda table: pltpu.with_memory_space_constraint(jnp.asarray(table), pltpu.HBM)
    first_table = jnp.asarray(first_tables())
    y_table = jnp.asarray(second_table())
    cross, odd_weight, *rows = depth_modes(
        place,
        ensemble,
        in_hbm(depth_tables()),
        in_hbm(obs_index.reshape(OBS_DEV // 128, 128)),
        in_hbm(obs_scale.reshape(OBS_DEV // 128, 128)),
    )
    cross = backwards(cross, "gy")
    rows = [rows[0]] + [shifted(rows[s], s) for s in range(1, GX)]
    even = first_modes(place, first_table, rows)
    odd = second_modes(place, y_table, cross)
    even = lax.all_to_all(even, "gy", split_axis=0, concat_axis=0, tiled=True)
    odd = [odd[0]] + [shifted(odd[s], s) for s in range(1, GX)]
    parts = gram(place, first_table, y_table, odd_weight, even, odd)
    parts = backwards(parts, "gx")
    parts = jnp.broadcast_to(jnp.sum(parts, axis=0), (GY, 24, 128))
    parts = backwards(parts, "gy")
    return analyse(parts, member_order.reshape(1, M), ensemble)


def solution(mesh):
    placed = (P(None, "gx", "gy"), P(("gx", "gy")), P(("gx", "gy")), P())
    return jax.shard_map(
        on_device, mesh=mesh, in_specs=placed, out_specs=P(None, "gx", "gy"), check_vma=False
    )
```
